256 devices in a mesh: chan: 32 (over y, x, z_hi), tm: 8 (over z_lo, core).
Axes of the slice: x: 4, y: 4, z: 8 (z_hi: 2, z_lo: 4; z = z_hi * 4 + z_lo), core: 2. Of those that a mesh axis runs over, the one named last changes fastest.
Arguments:
- spectra: bfloat16 [1024, 128, 2, 1024], P('chan', 'tm'), may hold values from -6 to 6
- quality: int32 [1024, 128], P('chan', 'tm'), may hold values from 0 to 1, as said below
- plan: int32 [3], replicated, may hold values from 0 to 31, as said below
Outputs:
- correlations: float32 [96, 1024, 2048], P('tm', 'chan')
The draws below stay inside these ranges and needn't reach their ends.
Inputs may be any that keep to these rules, and one draw needn't show every extreme that they name: `plan`: distinct channel block numbers; the first and the last block of the fibre are always among them. `quality`: 0 or 1; some channels are unusable in every segment.
All inputs are finite; a program needn't handle non-finite values.
Results may differ from the reference program's by a relative error of at most 0.0003.
Values may be sent and summed in bfloat16 or wider, within the bound.
A program may use at most 192 MiB of HBM per device.

```python
import math
import jax
import jax.numpy as jnp
from jax import lax

SRC_BLOCK = 32
SRC_BLOCKS = 3
CH_DEV = 32
BINS = 1024
LAGS = 2048
CHANNELS = 1024
SEGMENTS = 128
SOURCES = 96


def draw_quality(key, part):
    key_dead = jax.random.fold_in(key, 11)
    key_keep = jax.random.fold_in(key, 12)
    alive = jax.random.randint(key_dead, (CHANNELS,), 0, 16) != 0
    limit = 4 * (SEGMENTS - 1)
    rolled = jax.random.randint(key_keep, (CHANNELS, SEGMENTS), 0, limit)
    border = SEGMENTS - 1 + 2 * jnp.arange(SEGMENTS, dtype=jnp.int32)
    keep = rolled < border[None, :]
    return (alive[:, None] & keep).astype(jnp.int32)


def draw_plan(key, part):
    total = CHANNELS // SRC_BLOCK
    key_pick = jax.random.fold_in(key, 21)
    key_order = jax.random.fold_in(key, 22)
    middle = jax.random.permutation(key_pick, total - 2).astype(jnp.int32) + 1
    chosen = jnp.concatenate([jnp.array([0, total - 1], dtype=jnp.int32), middle[:SRC_BLOCKS - 2]])
    order = jax.random.permutation(key_order, SRC_BLOCKS)
    return chosen[order].astype(jnp.int32)


def block_levels(key, dims, split, smallest, high):
    gain = 1.0
    for axis_at, parts in split:
        steps = jax.random.uniform(jax.random.fold_in(jax.random.fold_in(key, 6), axis_at), (parts,), jnp.float32, smallest / len(split), high / len(split))
        gain = gain * jnp.repeat(jnp.exp(steps), dims[axis_at] // parts).reshape((-1,) + (1,) * (len(dims) - 1 - axis_at))
    return gain


def noise(own_key, extent, scale, most, cuts=(), kind=jnp.bfloat16):
    loudness = block_levels(own_key, extent, cuts, -0.22, 0.18) if cuts else 1.0
    values = jax.random.normal(own_key, extent, jnp.float32) * scale * loudness
    return jnp.minimum(jnp.maximum(values, -most), most).astype(kind)


def setup_inputs(seed: int = 0) -> dict:
    key_of = jax.random.split(jax.random.key(seed), 4)
    return {
        "spectra": noise(key_of[0], (CHANNELS, SEGMENTS, 2, BINS), 1.0, 6.0, ((0, 32), (1, 8))),
        "quality": draw_quality(jax.random.fold_in(key_of[3], 71), 0),
        "plan": draw_plan(jax.random.fold_in(key_of[3], 71), 0),
    }


def make_table(bins, lags):
    freq = lax.broadcasted_iota(jnp.int32, (bins, lags), 0)
    delay = lax.broadcasted_iota(jnp.int32, (bins, lags), 1) - bins
    phase = freq * delay % (2 * bins)
    angle = phase.astype(jnp.float32) * (math.pi / bins)
    scale = 1.0 / math.sqrt(bins)
    return jnp.concatenate([jnp.cos(angle) * scale, -jnp.sin(angle) * scale], axis=0)

def correlate(source, receiver):
    rotated = jnp.stack([receiver[:, :, 1], -receiver[:, :, 0]], axis=2)
    real_part = jnp.einsum('stpk,ctpk->sck', source, receiver)
    imag_part = jnp.einsum('stpk,ctpk->sck', source, rotated)
    return jnp.stack([real_part, imag_part], axis=2)

def reference(spectra, quality, plan):
    table = make_table(BINS, LAGS)
    offsets = jnp.arange(SRC_BLOCK, dtype=jnp.int32)
    groups = CHANNELS // CH_DEV
    flags_all = quality.astype(jnp.float32)

    def one_block(block):
        chosen = block * SRC_BLOCK + offsets
        source_flags = flags_all[chosen]
        source = spectra[chosen].astype(jnp.float32) * source_flags[:, :, None, None]

        def one_group(group):
            start = (group * CH_DEV).astype(jnp.int32)
            recv_spec = lax.dynamic_slice_in_dim(spectra, start, CH_DEV, 0).astype(jnp.float32)
            recv_flags = lax.dynamic_slice_in_dim(flags_all, start, CH_DEV, 0)
            receiver = recv_spec * recv_flags[:, :, None, None]
            cross = correlate(source, receiver)
            pair_count = jnp.dot(source_flags, recv_flags.T, precision=lax.Precision.HIGHEST, preferred_element_type=jnp.float32)
            stacked = cross / jnp.maximum(pair_count, 1.0)[:, :, None, None]
            flat = stacked.reshape(SRC_BLOCK * CH_DEV, 2 * BINS)
            result = jnp.dot(flat, table, precision=lax.Precision.HIGHEST, preferred_element_type=jnp.float32)
            return result.reshape(SRC_BLOCK, CH_DEV, LAGS)
        pieces = lax.map(one_group, jnp.arange(groups, dtype=jnp.int32))
        return jnp.transpose(pieces, (1, 0, 2, 3)).reshape(SRC_BLOCK, CHANNELS, LAGS)
    blocks = lax.map(one_block, plan.astype(jnp.int32))
    return blocks.reshape(SOURCES, CHANNELS, LAGS)
```

```python
import functools
import math

import jax
import jax.numpy as jnp
from jax import lax
from jax.experimental import pallas as pl
from jax.experimental.pallas import tpu as pltpu
from jax.sharding import PartitionSpec as P

MESH = pl.DeviceIdType.MESH
ANY = pl.ANY
SRC = 3
NX = NY = 4
NTM = 8
CH = 32
SEG = 16
BINS = 1024
KB = BINS // NTM
ROWS = SRC * KB + CH
BIG = 56 * 1024 * 1024


def place():
    ch = lax.axis_index("chan")
    return ch // 8, lax.rem(ch // 2, 4), lax.rem(ch, 2), lax.axis_index("tm")


def device(y, x, zh, tm):
    return ((y * 4 + x) * 2 + zh, tm)


def up(v, d):
    return lax.rem(v + d, 4)


def greet(devices):
    bar = pltpu.get_barrier_semaphore()
    for d in devices:
        pl.semaphore_signal(bar, inc=1, device_id=d, device_id_type=MESH)
    pl.semaphore_wait(bar, len(devices))


def remote(src, dst, send, recv, where):
    copy = pltpu.make_async_remote_copy(
        src_ref=src, dst_ref=dst, send_sem=send, recv_sem=recv, device_id=where, device_id_type=MESH
    )
    copy.start()
    return copy


def exchange_body(plan, m, y_out, rx, sx, ry, sy, rz, sh, send, recv, local):
    y, x, zh, tm = place()
    tms = [lax.rem(tm + d, NTM) for d in range(1, NTM)]
    greet(
        [device(y, x, zh, t) for t in tms]
        + [device(y, up(x, d), zh, tm) for d in (1, 2, 3)]
        + [device(up(y, d), x, zh, tm) for d in (1, 2, 3)]
        + [device(y, x, 1 - zh, tm)]
    )
    ox = [lax.rem(plan[b] // 2, 4) for b in range(SRC)]
    oy = [plan[b] // 8 for b in range(SRC)]
    oz = [lax.rem(plan[b], 2) for b in range(SRC)]

    stage_x = []
    for d in (1, 3, 2):
        to = up(x, d)
        stage_x.append(
            remote(m.at[pl.ds(to * 8, 8)], rx.at[x], send.at[d], recv.at[d], device(y, to, zh, tm))
        )
    own_x = pltpu.make_async_copy(m.at[pl.ds(x * 8, 8)], rx.at[x], local.at[0])
    own_x.start()
    main = []
    for d in range(1, NTM):
        t = tms[d - 1]
        lanes = pl.ds(pl.multiple_of(t * KB, KB), KB)
        rows = pl.ds(pl.multiple_of(tm * SEG, SEG), SEG)
        main.append(
            remote(
                m.at[:, :, :, lanes],
                y_out.at[pl.ds(0, CH + 1), :, rows, :],
                send.at[8 + d],
                recv.at[8 + d],
                device(y, x, zh, t),
            )
        )
    my_lanes = pl.ds(pl.multiple_of(tm * KB, KB), KB)
    my_rows = pl.ds(pl.multiple_of(tm * SEG, SEG), SEG)
    own_m = pltpu.make_async_copy(
        m.at[:, :, :, my_lanes], y_out.at[pl.ds(0, CH + 1), :, my_rows, :], local.at[1]
    )
    own_m.start()

    own_x.wait()
    for c in stage_x:
        c.wait_recv()
    for b in range(SRC):

        def pick_x(i, carry, b=b):
            sx[b, i] = rx[ox[b], i]
            return carry

        lax.fori_loop(0, 8, pick_x, 0)
    stage_y = []
    for d in (1, 3, 2):
        to = up(y, d)
        stage_y.append(
            remote(
                sx.at[:, pl.ds(to * 2, 2)],
                ry.at[y],
                send.at[4 + d],
                recv.at[4 + d],
                device(to, x, zh, tm),
            )
        )
    own_y = pltpu.make_async_copy(sx.at[:, pl.ds(y * 2, 2)], ry.at[y], local.at[2])
    own_y.start()
    own_y.wait()
    for c in stage_y:
        c.wait_recv()
    for b in range(SRC):

        def pick_y(i, carry, b=b):
            sy[i, b] = ry[oy[b], b, i]
            return carry

        lax.fori_loop(0, 2, pick_y, 0)
    stage_z = remote(sy.at[1 - zh], rz.at[zh], send.at[0], recv.at[0], device(y, x, 1 - zh, tm))
    own_z = pltpu.make_async_copy(sy.at[zh], rz.at[zh], local.at[3])
    own_z.start()
    own_z.wait()
    stage_z.wait_recv()
    for b in range(SRC):
        sh[b] = rz[oz[b], b]
    shares = []
    for d in range(1, NTM):
        t = tms[d - 1]
        lanes = pl.ds(pl.multiple_of(t * KB, KB), KB)
        shares.append(
            remote(
                sh.at[:, :, :, lanes],
                y_out.at[pl.ds(CH + 1, SRC), :, my_rows, :],
                send.at[16 + d],
                recv.at[16 + d],
                device(y, x, zh, t),
            )
        )
    own_s = pltpu.make_async_copy(
        sh.at[:, :, :, my_lanes], y_out.at[pl.ds(CH + 1, SRC), :, my_rows, :], local.at[4]
    )
    own_s.start()
    own_s.wait()
    own_m.wait()
    for c in stage_x + stage_y + [stage_z]:
        c.wait_send()
    for c in main + shares:
        c.wait()


def exchange(plan, m):
    bf = jnp.bfloat16
    return pl.pallas_call(
        exchange_body,
        out_shape=jax.ShapeDtypeStruct((CH + 1 + SRC, 2, NTM * SEG, KB), bf),
        in_specs=[pl.BlockSpec(memory_space=pltpu.SMEM), pl.BlockSpec(memory_space=ANY)],
        out_specs=pl.BlockSpec(memory_space=ANY),
        scratch_shapes=[
            pltpu.VMEM((4, 8, 2, SEG, BINS), bf),
            pltpu.VMEM((SRC, 8, 2, SEG, BINS), bf),
            pltpu.VMEM((4, SRC, 2, 2, SEG, BINS), bf),
            pltpu.VMEM((2, SRC, 2, SEG, BINS), bf),
            pltpu.VMEM((2, SRC, 2, SEG, BINS), bf),
            pltpu.VMEM((SRC, 2, SEG, BINS), bf),
            pltpu.SemaphoreType.DMA((24,)),
            pltpu.SemaphoreType.DMA((24,)),
            pltpu.SemaphoreType.DMA((5,)),
        ],
        compiler_params=pltpu.CompilerParams(
            collective_id=0, has_side_effects=True, vmem_limit_bytes=BIG
        ),
    )(plan, m)


def share_body(y_ref, s_ref):
    for b in range(SRC):
        for p in range(2):
            s_ref[pl.ds(b * KB, KB), pl.ds(p * 128, 128)] = (
                y_ref[1 + b, p].astype(jnp.float32).T.astype(jnp.bfloat16)
            )
    for p in range(2):
        flags = y_ref[0, p].astype(jnp.float32).T[:CH]
        s_ref[pl.ds(SRC * KB, CH), pl.ds(p * 128, 128)] = flags.astype(jnp.bfloat16)


def share(y):
    return pl.pallas_call(
        share_body,
        grid=(1,),
        out_shape=jax.ShapeDtypeStruct((ROWS, 256), jnp.bfloat16),
        in_specs=[pl.BlockSpec((4, 2, 128, KB), lambda g: (8, 0, 0, 0))],
        out_specs=pl.BlockSpec((ROWS, 256), lambda g: (0, 0)),
    )(y)


def gather_body(s_ref, o_ref, send, recv, local):
    y, x, zh, tm = place()
    near = [
        device(y, up(x, 1), zh, tm),
        device(y, up(x, 3), zh, tm),
        device(up(y, 1), x, zh, tm),
        device(up(y, 3), x, zh, tm),
        device(y, x, 1 - zh, tm),
    ]
    greet(near)
    cut = ROWS // 32 * 16
    me = y * 4 + x
    own = pltpu.make_async_copy(s_ref, o_ref.at[zh, me], local)
    own.start()
    across = remote(s_ref, o_ref.at[zh, me], send.at[0], recv.at[0], near[4])
    started = []
    full, low, high = pl.ds(0, ROWS), pl.ds(0, cut), pl.ds(cut, ROWS - cut)

    def put(half, slot, part, k, where):
        ref = o_ref.at[half, slot, part]
        copy = remote(ref, ref, send.at[k], recv.at[k], where)
        started.append(copy)
        return copy

    class Half:
        def __init__(self, half):
            self.half = half
            first, second = (near[:2], near[2:4]) if half == 0 else (near[2:4], near[:2])
            self.ap, self.am = first
            self.bp, self.bm = second
            self.a, self.b = (x, y) if half == 0 else (y, x)
            self.base = 1 + 20 * half
            self.sent = {}
            self.passed = {}

        def slot(self, b, a):
            return b * 4 + a if self.half == 0 else a * 4 + b

        def at(self, r):
            return up(self.a, (0, 3, 1, 2)[r])

        def send_b(self, r):
            k = self.base + 4 + 4 * r
            slot = self.slot(self.b, self.at(r))
            self.sent[r] = (
                put(self.half, slot, full, k, self.bp),
                put(self.half, slot, full, k + 1, self.bm),
            )

        def start(self):
            slot = self.slot(self.b, self.a)
            self.a1 = put(self.half, slot, full, self.base, self.ap)
            self.a2 = put(self.half, slot, full, self.base + 1, self.am)
            self.send_b(0)

        def first(self):
            self.a1.wait_recv()
            self.a3 = put(self.half, self.slot(self.b, self.at(1)), low, self.base + 2, self.ap)
            self.send_b(1)
            self.a2.wait_recv()
            self.a4 = put(self.half, self.slot(self.b, self.at(2)), high, self.base + 3, self.am)
            self.send_b(2)

        def second(self):
            self.a3.wait_recv()
            self.a4.wait_recv()
            self.send_b(3)

        def forward(self, r):
            k = self.base + 4 + 4 * r
            a = self.at(r)
            plus, minus = self.sent[r]
            plus.wait_recv()
            f1 = put(self.half, self.slot(up(self.b, 3), a), low, k + 2, self.bp)
            minus.wait_recv()
            f2 = put(self.half, self.slot(up(self.b, 1), a), high, k + 3, self.bm)
            self.passed[r] = (f1, f2)

    own.wait()
    across.wait_recv()
    halves = [Half(0), Half(1)]
    for h in halves:
        h.start()
    for h in halves:
        h.first()
    for h in halves:
        h.forward(0)
    for h in halves:
        h.second()
    for r in (1, 2, 3):
        for h in halves:
            h.forward(r)
    for r in range(4):
        for h in halves:
            for f in h.passed[r]:
                f.wait_recv()
    across.wait_send()
    for copy in started:
        copy.wait_send()


def gather(s):
    return pl.pallas_call(
        gather_body,
        out_shape=jax.ShapeDtypeStruct((2, 16, ROWS, 256), jnp.bfloat16),
        in_specs=[pl.BlockSpec(memory_space=ANY)],
        out_specs=pl.BlockSpec(memory_space=ANY),
        scratch_shapes=[
            pltpu.SemaphoreType.DMA((41,)),
            pltpu.SemaphoreType.DMA((41,)),
            pltpu.SemaphoreType.DMA,
        ],
        compiler_params=pltpu.CompilerParams(collective_id=1, has_side_effects=True),
    )(s)


def correlate_body(plan, g_ref, y_ref, out_ref, sa, sq, ra, rq, ob):
    f32, bf = jnp.float32, jnp.bfloat16

    def widen(j, carry):
        zh, y, x = lax.rem(j, 2), lax.rem(j // 2, 4), j // 8
        for b in range(SRC):
            rows = pl.ds(pl.multiple_of((b * CH + j) * KB, KB), KB)
            for p, part in enumerate((sa, sq)):
                lanes = pl.ds(p * 128, 128)
                part[rows, :] = g_ref[zh, y * 4 + x, pl.ds(b * KB, KB), lanes].astype(f32)
        rows = pl.ds(pl.multiple_of(j * KB, KB), KB)
        for p, part in enumerate((ra, rq)):
            part[rows, :] = y_ref[j, p].astype(f32).T
        return carry

    lax.fori_loop(0, CH, widen, 0)
    fr = y_ref[CH, 0].astype(f32).T[:CH]
    fr = jnp.concatenate([fr, fr], axis=0).astype(bf)
    counts = []
    for b in range(SRC):
        fs = g_ref[lax.rem(plan[b], 2), plan[b] // 2, pl.ds(SRC * KB, CH), pl.ds(0, 128)]
        counts.append(
            lax.dot_general(fs, fr, (((1,), (1,)), ((), ())), preferred_element_type=f32)
        )
    inverse = 1.0 / jnp.maximum(jnp.concatenate(counts, axis=0), 1.0)

    def one(k):
        sources, channels = pl.ds(k, SRC * CH, stride=KB), pl.ds(k, CH, stride=KB)
        s = jnp.concatenate([sa[sources, :], sq[sources, :]], axis=1).astype(bf)
        a, q = ra[channels, :], rq[channels, :]
        real, imag = jnp.concatenate([a, q], axis=1), jnp.concatenate([q, -a], axis=1)
        both = jnp.concatenate([real, imag], axis=0).astype(bf)
        res = lax.dot_general(s, both, (((1,), (1,)), ((), ())), preferred_element_type=f32)
        res = res * inverse
        ob[sources, :] = jnp.concatenate([res, jnp.zeros_like(res)], axis=1)

    def some(i, carry):
        for u in range(8):
            one(i * 8 + u)
        return carry

    lax.fori_loop(0, KB // 8, some, 0)

    def turn(i, carry):
        for u in range(4):
            s = i * 4 + u
            out_ref[s] = ob[pl.ds(pl.multiple_of(s * KB, KB), KB), pl.ds(0, 2 * CH)].T
        return carry

    lax.fori_loop(0, SRC * CH // 4, turn, 0)


def correlate(plan, g, y):
    vmem = pl.BlockSpec(memory_space=pltpu.VMEM)
    return pl.pallas_call(
        correlate_body,
        out_shape=jax.ShapeDtypeStruct((SRC * CH, 2 * CH, KB), jnp.float32),
        in_specs=[pl.BlockSpec(memory_space=pltpu.SMEM), vmem, vmem],
        out_specs=vmem,
        scratch_shapes=[
            pltpu.VMEM((SRC * CH * KB, 128), jnp.float32),
            pltpu.VMEM((SRC * CH * KB, 128), jnp.float32),
            pltpu.VMEM((CH * KB, 128), jnp.float32),
            pltpu.VMEM((CH * KB, 128), jnp.float32),
            pltpu.VMEM((SRC * CH * KB, 128), jnp.float32),
        ],
        compiler_params=pltpu.CompilerParams(vmem_limit_bytes=BIG),
    )(plan, g, y)


def collect_body(x_ref, v_ref, send, recv, local):
    y, x, zh, tm = place()
    tms = [lax.rem(tm + d, NTM) for d in range(1, NTM)]
    greet([device(y, x, zh, t) for t in tms])
    copies = []
    for d in range(1, NTM):
        t = tms[d - 1]
        copies.append(
            remote(x_ref.at[t], v_ref.at[tm], send.at[d], recv.at[d], device(y, x, zh, t))
        )
    own = pltpu.make_async_copy(x_ref.at[tm], v_ref.at[tm], local)
    own.start()
    own.wait()
    for c in copies:
        c.wait()


def collect(x):
    return pl.pallas_call(
        collect_body,
        out_shape=jax.ShapeDtypeStruct(x.shape, x.dtype),
        in_specs=[pl.BlockSpec(memory_space=ANY)],
        out_specs=pl.BlockSpec(memory_space=ANY),
        scratch_shapes=[
            pltpu.SemaphoreType.DMA((NTM,)),
            pltpu.SemaphoreType.DMA((NTM,)),
            pltpu.SemaphoreType.DMA,
        ],
        compiler_params=pltpu.CompilerParams(collective_id=2, has_side_effects=True),
    )(x)


def make_table():
    tau = lax.broadcasted_iota(jnp.int32, (1, 2 * BINS), 1) - BINS

    def pair(count, step):
        freq = lax.broadcasted_iota(jnp.int32, (count, 1), 0) * step
        angle = ((freq * tau) % (2 * BINS)).astype(jnp.float32) * (math.pi / BINS)
        return jnp.cos(angle), jnp.sin(angle)

    c1, s1 = (v[:, None, :] for v in pair(BINS // 8, 8))
    c2, s2 = (v[None, :, :] / math.sqrt(BINS) for v in pair(8, 1))
    shape = (BINS, 2 * BINS)
    table = jnp.concatenate(
        [(c1 * c2 - s1 * s2).reshape(shape), -(s1 * c2 + c1 * s2).reshape(shape)], axis=0
    )
    high = lax.reduce_precision(table, 8, 7)
    return high.astype(jnp.bfloat16), (table - high).astype(jnp.bfloat16)


def lags_body(v_ref, th_ref, tl_ref, out_ref, xh, xl):
    @pl.when(pl.program_id(0) == 0)
    def _():
        def split(s, carry):
            rows = pl.ds(pl.multiple_of(s * CH, CH), CH)
            for p in range(2):
                for j in range(NTM):
                    lanes = pl.ds(p * BINS + j * KB, KB)
                    value = v_ref[j, s, p]
                    high = value.astype(jnp.bfloat16)
                    xh[rows, lanes] = high
                    xl[rows, lanes] = (value - high.astype(jnp.float32)).astype(jnp.bfloat16)
            return carry

        lax.fori_loop(0, 12, split, 0)

    def dot(a, b):
        return jnp.dot(a, b, preferred_element_type=jnp.float32)

    th = th_ref[...]
    h = xh[...]
    out_ref[...] = dot(xl[...], th) + dot(h, tl_ref[...]) + dot(h, th)


def lags(v, th, tl):
    rows, wide, step = 12 * CH, 2 * BINS, 256
    return pl.pallas_call(
        lags_body,
        grid=(wide // step,),
        out_shape=jax.ShapeDtypeStruct((rows, wide), jnp.float32),
        in_specs=[
            pl.BlockSpec((NTM, 12, 2, CH, KB), lambda g: (0, 0, 0, 0, 0)),
            pl.BlockSpec((wide, step), lambda g: (0, g)),
            pl.BlockSpec((wide, step), lambda g: (0, g)),
        ],
        out_specs=pl.BlockSpec((rows, step), lambda g: (0, g)),
        scratch_shapes=[
            pltpu.VMEM((rows, wide), jnp.bfloat16),
            pltpu.VMEM((rows, wide), jnp.bfloat16),
        ],
        compiler_params=pltpu.CompilerParams(vmem_limit_bytes=BIG),
    )(v, th, tl)


def shards(spectra, quality, plan):
    flags = quality.astype(jnp.bfloat16)
    masked = (spectra * flags[:, :, None, None]).transpose(0, 2, 1, 3)
    row = jnp.tile(jnp.pad(flags.T, ((0, 0), (0, KB - CH))), (1, NTM))
    m = jnp.concatenate([masked, jnp.broadcast_to(row, (1, 2, SEG, BINS))], axis=0)
    th, tl = make_table()
    y = exchange(plan, m)
    g = gather(share(y))
    x = correlate(plan, g, y)
    v = collect(x.reshape(NTM, 12 * 2 * CH, KB))
    out = lags(v.reshape(NTM, 12, 2, CH, KB), th, tl)
    return out.reshape(12, CH, 2 * BINS)


def solution(mesh):
    in_specs = (P("chan", "tm", None, None), P("chan", "tm"), P())
    out_specs = P("tm", "chan", None)
    return jax.shard_map(shards, mesh=mesh, in_specs=in_specs, out_specs=out_specs, check_vma=False)
```

```python
import functools
import math

import jax
import jax.numpy as jnp
from jax import lax
from jax.experimental import pallas as pl
from jax.experimental.pallas import tpu as pltpu
from jax.sharding import PartitionSpec as P

MESH = pl.DeviceIdType.MESH
ANY = pl.ANY
SRC = 3
NX = NY = 4
NTM = 8
CH = 32
SEG = 16
BINS = 1024
KB = BINS // NTM
ROWS = SRC * KB + CH
EARLY = 16
TOP = 32766.0
BIG = 56 * 1024 * 1024


def place():
    ch = lax.axis_index("chan")
    return ch // 8, lax.rem(ch // 2, 4), lax.rem(ch, 2), lax.axis_index("tm")


def device(y, x, zh, tm):
    return ((y * 4 + x) * 2 + zh, tm)


def up(v, d):
    return lax.rem(v + d, 4)


def greet(devices):
    bar = pltpu.get_barrier_semaphore()
    for d in devices:
        pl.semaphore_signal(bar, inc=1, device_id=d, device_id_type=MESH)
    pl.semaphore_wait(bar, len(devices))


def remote(src, dst, send, recv, where):
    copy = pltpu.make_async_remote_copy(
        src_ref=src, dst_ref=dst, send_sem=send, recv_sem=recv, device_id=where, device_id_type=MESH
    )
    copy.start()
    return copy


def front_body(plan, m, y_out, o_ref, rx, sx, ry, sy, rz, sh, yb, own_share, send, recv, local):
    y, x, zh, tm = place()
    tms = [lax.rem(tm + d, NTM) for d in range(1, NTM)]
    greet(
        [device(y, x, zh, t) for t in tms]
        + [device(y, up(x, d), zh, tm) for d in (1, 2, 3)]
        + [device(up(y, d), x, zh, tm) for d in (1, 2, 3)]
        + [device(y, x, 1 - zh, tm)]
    )
    ox = [lax.rem(plan[b] // 2, 4) for b in range(SRC)]
    oy = [plan[b] // 8 for b in range(SRC)]
    oz = [lax.rem(plan[b], 2) for b in range(SRC)]
    my_lanes = pl.ds(pl.multiple_of(tm * KB, KB), KB)
    my_rows = pl.ds(pl.multiple_of(tm * SEG, SEG), SEG)

    def bins_of(t):
        return pl.ds(pl.multiple_of(t * KB, KB), KB)

    def main(first, count, base):
        return [
            remote(
                m.at[pl.ds(first, count), :, :, bins_of(tms[d - 1])],
                y_out.at[pl.ds(first, count), :, my_rows, :],
                send.at[base + d],
                recv.at[base + d],
                device(y, x, zh, tms[d - 1]),
            )
            for d in range(1, NTM)
        ]

    stage_x = []
    for d in (1, 3, 2):
        to = up(x, d)
        stage_x.append(
            remote(m.at[pl.ds(to * 8, 8)], rx.at[x], send.at[d], recv.at[d], device(y, to, zh, tm))
        )
    own_x = pltpu.make_async_copy(m.at[pl.ds(x * 8, 8)], rx.at[x], local.at[0])
    own_x.start()
    own_f = pltpu.make_async_copy(m.at[CH], sh.at[0], local.at[5])
    own_f.start()
    exchanged = main(0, EARLY, 8)
    own_m = pltpu.make_async_copy(
        m.at[pl.ds(0, CH), :, :, my_lanes], y_out.at[:, :, my_rows, :], local.at[1]
    )
    own_m.start()

    own_x.wait()
    for c in stage_x:
        c.wait_recv()
    for b in range(SRC):

        def pick_x(i, carry, b=b):
            sx[b, i] = rx[ox[b], i]
            return carry

        lax.fori_loop(0, 8, pick_x, 0)
    stage_y = []
    for d in (1, 3, 2):
        to = up(y, d)
        stage_y.append(
            remote(
                sx.at[:, pl.ds(to * 2, 2)],
                ry.at[y],
                send.at[4 + d],
                recv.at[4 + d],
                device(to, x, zh, tm),
            )
        )
    own_y = pltpu.make_async_copy(sx.at[:, pl.ds(y * 2, 2)], ry.at[y], local.at[2])
    own_y.start()
    own_y.wait()
    for c in stage_y:
        c.wait_recv()
    for b in range(SRC):

        def pick_y(i, carry, b=b):
            sy[i, b] = ry[oy[b], b, i]
            return carry

        lax.fori_loop(0, 2, pick_y, 0)
    stage_z = remote(sy.at[1 - zh], rz.at[zh], send.at[0], recv.at[0], device(y, x, 1 - zh, tm))
    own_z = pltpu.make_async_copy(sy.at[zh], rz.at[zh], local.at[3])
    own_z.start()
    own_z.wait()
    stage_z.wait_recv()
    own_f.wait()
    for b in range(SRC):
        sh[1 + b] = rz[oz[b], b]
    shares = [
        remote(
            sh.at[:, :, :, bins_of(tms[d - 1])],
            yb.at[:, :, my_rows, :],
            send.at[16 + d],
            recv.at[16 + d],
            device(y, x, zh, tms[d - 1]),
        )
        for d in range(1, NTM)
    ]
    own_s = pltpu.make_async_copy(sh.at[:, :, :, my_lanes], yb.at[:, :, my_rows, :], local.at[4])
    own_s.start()
    exchanged += main(EARLY, CH - EARLY, 24)
    own_s.wait()
    for c in shares:
        c.wait_recv()

    def turned(i, p):
        return yb[i, p].astype(jnp.float32).T

    for p in range(2):
        lanes = pl.ds(p * 128, 128)
        for b in range(SRC):
            own_share[pl.ds(b * KB, KB), lanes] = turned(1 + b, p).astype(jnp.bfloat16)
        own_share[pl.ds(SRC * KB, CH), lanes] = turned(0, p)[:CH].astype(jnp.bfloat16)

    cut = ROWS // 32 * 16
    me = y * 4 + x
    across = remote(
        own_share, o_ref.at[zh, me], send.at[32], recv.at[32], device(y, x, 1 - zh, tm)
    )
    own = pltpu.make_async_copy(own_share, o_ref.at[zh, me], local.at[6])
    own.start()
    started = []
    full, low, high = pl.ds(0, ROWS), pl.ds(0, cut), pl.ds(cut, ROWS - cut)

    class Half:
        def __init__(self, half):
            self.half = half
            ay, ax = half, 1 - half
            self.ap = device(up(y, ay), up(x, ax), zh, tm)
            self.am = device(up(y, 3 * ay), up(x, 3 * ax), zh, tm)
            self.bp = device(up(y, ax), up(x, ay), zh, tm)
            self.bm = device(up(y, 3 * ax), up(x, 3 * ay), zh, tm)
            self.a = x * ax + y * ay
            self.b = x * ay + y * ax
            self.base = 33 + 20 * half
            self.sent = {}
            self.passed = {}

        def put(self, b, a, part, k, where, source=None):
            slot = b * (4 - 3 * self.half) + a * (1 + 3 * self.half)
            ref = o_ref.at[self.half, slot, part]
            k = self.base + k
            copy = remote(ref if source is None else source, ref, send.at[k], recv.at[k], where)
            started.append(copy)
            return copy

        def at(self, r):
            return up(self.a, (0, 3, 1, 2)[r])

        def send_b(self, r, source=None):
            k = 4 + 4 * r
            self.sent[r] = (
                self.put(self.b, self.at(r), full, k, self.bp, source),
                self.put(self.b, self.at(r), full, k + 1, self.bm, source),
            )

        def start(self, source=None):
            self.a1 = self.put(self.b, self.a, full, 0, self.ap, source)
            self.a2 = self.put(self.b, self.a, full, 1, self.am, source)
            self.send_b(0, source)

        def first(self):
            self.a1.wait_recv()
            self.a3 = self.put(self.b, self.at(1), low, 2, self.ap)
            self.send_b(1)
            self.a2.wait_recv()
            self.a4 = self.put(self.b, self.at(2), high, 3, self.am)
            self.send_b(2)

        def second(self):
            self.a3.wait_recv()
            self.a4.wait_recv()
            self.send_b(3)

        def forward(self, r):
            k = 4 + 4 * r
            plus, minus = self.sent[r]
            plus.wait_recv()
            f1 = self.put(up(self.b, 3), self.at(r), low, k + 2, self.bp)
            minus.wait_recv()
            f2 = self.put(up(self.b, 1), self.at(r), high, k + 3, self.bm)
            self.passed[r] = (f1, f2)

    mine, other = Half(zh), Half(1 - zh)
    mine.start(own_share)
    mine.first()
    across.wait_recv()
    other.start()
    mine.forward(0)
    mine.second()
    other.first()
    mine.forward(1)
    other.forward(0)
    mine.forward(2)
    other.second()
    mine.forward(3)
    for r in (1, 2, 3):
        other.forward(r)
    for r in range(4):
        for h in (mine, other):
            for f in h.passed[r]:
                f.wait_recv()
    own.wait()
    own_m.wait()
    for c in exchanged:
        c.wait_recv()
    for c in stage_x + stage_y + [stage_z, across] + shares + exchanged + started:
        c.wait_send()


def front(plan, m):
    bf = jnp.bfloat16
    return pl.pallas_call(
        front_body,
        out_shape=(
            jax.ShapeDtypeStruct((CH, 2, NTM * SEG, KB), bf),
            jax.ShapeDtypeStruct((2, 16, ROWS, 256), bf),
        ),
        in_specs=[pl.BlockSpec(memory_space=pltpu.SMEM), pl.BlockSpec(memory_space=ANY)],
        out_specs=(pl.BlockSpec(memory_space=ANY), pl.BlockSpec(memory_space=ANY)),
        scratch_shapes=[
            pltpu.VMEM((4, 8, 2, SEG, BINS), bf),
            pltpu.VMEM((SRC, 8, 2, SEG, BINS), bf),
            pltpu.VMEM((4, SRC, 2, 2, SEG, BINS), bf),
            pltpu.VMEM((2, SRC, 2, SEG, BINS), bf),
            pltpu.VMEM((2, SRC, 2, SEG, BINS), bf),
            pltpu.VMEM((1 + SRC, 2, SEG, BINS), bf),
            pltpu.VMEM((1 + SRC, 2, NTM * SEG, KB), bf),
            pltpu.VMEM((ROWS, 256), bf),
            pltpu.SemaphoreType.DMA((73,)),
            pltpu.SemaphoreType.DMA((73,)),
            pltpu.SemaphoreType.DMA((7,)),
        ],
        compiler_params=pltpu.CompilerParams(
            collective_id=0, has_side_effects=True, vmem_limit_bytes=BIG
        ),
    )(plan, m)


def correlate_body(plan, g_ref, y_ref, out_ref, scale_ref, sa, sq, ra, rq, ob):
    f32, bf = jnp.float32, jnp.bfloat16

    def widen(j, carry):
        zh, y, x = lax.rem(j, 2), lax.rem(j // 2, 4), j // 8
        for b in range(SRC):
            rows = pl.ds(pl.multiple_of((b * CH + j) * KB, KB), KB)
            for p, part in enumerate((sa, sq)):
                lanes = pl.ds(p * 128, 128)
                part[rows, :] = g_ref[zh, y * 4 + x, pl.ds(b * KB, KB), lanes].astype(f32)
        rows = pl.ds(pl.multiple_of(j * KB, KB), KB)
        for p, part in enumerate((ra, rq)):
            part[rows, :] = y_ref[j, p].astype(f32).T
        return carry

    lax.fori_loop(0, CH, widen, 0)

    def flags(block):
        return g_ref[lax.rem(block, 2), block // 2, pl.ds(SRC * KB, CH), pl.ds(0, 128)]

    fr = flags(lax.axis_index("chan"))
    fr = jnp.concatenate([fr, fr], axis=0)
    counts = []
    for b in range(SRC):
        fs = flags(plan[b])
        counts.append(
            lax.dot_general(fs, fr, (((1,), (1,)), ((), ())), preferred_element_type=f32)
        )
    inverse = 1.0 / jnp.maximum(jnp.concatenate(counts, axis=0), 1.0)

    def one(k):
        sources, channels = pl.ds(k, SRC * CH, stride=KB), pl.ds(k, CH, stride=KB)
        s = jnp.concatenate([sa[sources, :], sq[sources, :]], axis=1).astype(bf)
        a, q = ra[channels, :], rq[channels, :]
        real, imag = jnp.concatenate([a, q], axis=1), jnp.concatenate([q, -a], axis=1)
        both = jnp.concatenate([real, imag], axis=0).astype(bf)
        res = lax.dot_general(s, both, (((1,), (1,)), ((), ())), preferred_element_type=f32)
        res = res * inverse
        ob[sources, :] = jnp.concatenate([res, jnp.zeros_like(res)], axis=1)

    def some(i, carry):
        for u in range(8):
            one(i * 8 + u)
        return carry

    lax.fori_loop(0, KB // 8, some, 0)

    def turn(t, carry):
        for i in range(12):
            s = t * 12 + i
            block = ob[pl.ds(pl.multiple_of(s * KB, KB), KB), pl.ds(0, 2 * CH)].T
            most = jnp.maximum(jnp.max(jnp.abs(block), axis=0, keepdims=True), 1e-30)
            code = jnp.round(block * (TOP / most)).astype(jnp.int32)
            out_ref[s] = code.astype(jnp.int16)
            scale_ref[t, pl.ds(i, 1), :] = most * (1.0 / TOP)
        return carry

    lax.fori_loop(0, NTM, turn, 0)


def correlate(plan, g, y):
    vmem = pl.BlockSpec(memory_space=pltpu.VMEM)
    return pl.pallas_call(
        correlate_body,
        out_shape=(
            jax.ShapeDtypeStruct((SRC * CH, 2 * CH, KB), jnp.int16),
            jax.ShapeDtypeStruct((NTM, 16, KB), jnp.float32),
        ),
        in_specs=[pl.BlockSpec(memory_space=pltpu.SMEM), vmem, vmem],
        out_specs=(vmem, vmem),
        scratch_shapes=[
            pltpu.VMEM((SRC * CH * KB, 128), jnp.float32),
            pltpu.VMEM((SRC * CH * KB, 128), jnp.float32),
            pltpu.VMEM((CH * KB, 128), jnp.float32),
            pltpu.VMEM((CH * KB, 128), jnp.float32),
            pltpu.VMEM((SRC * CH * KB, 128), jnp.float32),
        ],
        compiler_params=pltpu.CompilerParams(vmem_limit_bytes=BIG),
    )(plan, g, y)


def collect_body(x_ref, c_ref, v_ref, d_ref, send, recv, local):
    y, x, zh, tm = place()
    tms = [lax.rem(tm + d, NTM) for d in range(1, NTM)]
    greet([device(y, x, zh, t) for t in tms])
    copies = []
    for d in range(1, NTM):
        t = tms[d - 1]
        for i, (src, dst) in enumerate(((x_ref, v_ref), (c_ref, d_ref))):
            copies.append(
                remote(src.at[t], dst.at[tm], send.at[i, d], recv.at[i, d], device(y, x, zh, t))
            )
    own = [
        pltpu.make_async_copy(src.at[tm], dst.at[tm], local.at[i])
        for i, (src, dst) in enumerate(((x_ref, v_ref), (c_ref, d_ref)))
    ]
    for c in own:
        c.start()
    for c in own + copies:
        c.wait()


def collect(x, c):
    hbm = pl.BlockSpec(memory_space=ANY)
    return pl.pallas_call(
        collect_body,
        out_shape=(
            jax.ShapeDtypeStruct(x.shape, x.dtype),
            jax.ShapeDtypeStruct(c.shape, c.dtype),
        ),
        in_specs=[hbm, hbm],
        out_specs=(hbm, hbm),
        scratch_shapes=[
            pltpu.SemaphoreType.DMA((2, NTM)),
            pltpu.SemaphoreType.DMA((2, NTM)),
            pltpu.SemaphoreType.DMA((2,)),
        ],
        compiler_params=pltpu.CompilerParams(collective_id=2, has_side_effects=True),
    )(x, c)


def make_table():
    tau = lax.broadcasted_iota(jnp.int32, (1, 2 * BINS), 1) - BINS

    def pair(count, step):
        freq = lax.broadcasted_iota(jnp.int32, (count, 1), 0) * step
        angle = ((freq * tau) % (2 * BINS)).astype(jnp.float32) * (math.pi / BINS)
        return jnp.cos(angle), jnp.sin(angle)

    c1, s1 = (v[:, None, :] for v in pair(BINS // 8, 8))
    c2, s2 = (v[None, :, :] / math.sqrt(BINS) for v in pair(8, 1))
    shape = (BINS, 2 * BINS)
    table = jnp.concatenate(
        [(c1 * c2 - s1 * s2).reshape(shape), -(s1 * c2 + c1 * s2).reshape(shape)], axis=0
    )
    high = lax.reduce_precision(table, 8, 7)
    return high.astype(jnp.bfloat16), (table - high).astype(jnp.bfloat16)


def lags_body(v_ref, c_ref, th_ref, tl_ref, out_ref, xh, xl):
    @pl.when(pl.program_id(0) == 0)
    def _():
        def split(s, carry):
            rows = pl.ds(pl.multiple_of(s * CH, CH), CH)
            for p in range(2):
                for j in range(NTM):
                    lanes = pl.ds(p * BINS + j * KB, KB)
                    value = v_ref[j, s, p].astype(jnp.int32).astype(jnp.float32)
                    value = value * c_ref[j, pl.ds(s, 1), :]
                    high = value.astype(jnp.bfloat16)
                    xh[rows, lanes] = high
                    xl[rows, lanes] = (value - high.astype(jnp.float32)).astype(jnp.bfloat16)
            return carry

        lax.fori_loop(0, 12, split, 0)

    def dot(a, b):
        return jnp.dot(a, b, preferred_element_type=jnp.float32)

    th = th_ref[...]
    h = xh[...]
    out_ref[...] = dot(xl[...], th) + dot(h, tl_ref[...]) + dot(h, th)


def lags(v, c, th, tl):
    rows, wide, step = 12 * CH, 2 * BINS, 256
    return pl.pallas_call(
        lags_body,
        grid=(wide // step,),
        out_shape=jax.ShapeDtypeStruct((rows, wide), jnp.float32),
        in_specs=[
            pl.BlockSpec((NTM, 12, 2, CH, KB), lambda g: (0, 0, 0, 0, 0)),
            pl.BlockSpec((NTM, 16, KB), lambda g: (0, 0, 0)),
            pl.BlockSpec((wide, step), lambda g: (0, g)),
            pl.BlockSpec((wide, step), lambda g: (0, g)),
        ],
        out_specs=pl.BlockSpec((rows, step), lambda g: (0, g)),
        scratch_shapes=[
            pltpu.VMEM((rows, wide), jnp.bfloat16),
            pltpu.VMEM((rows, wide), jnp.bfloat16),
        ],
        compiler_params=pltpu.CompilerParams(vmem_limit_bytes=BIG),
    )(v, c, th, tl)


def shards(spectra, quality, plan):
    flags = quality.astype(jnp.bfloat16)
    masked = (spectra * flags[:, :, None, None]).transpose(0, 2, 1, 3)
    row = jnp.tile(jnp.pad(flags.T, ((0, 0), (0, KB - CH))), (1, NTM))
    m = jnp.concatenate([masked, jnp.broadcast_to(row, (1, 2, SEG, BINS))], axis=0)
    th, tl = make_table()
    y, g = front(plan, m)
    x, c = correlate(plan, g, y)
    v, c = collect(x.reshape(NTM, 12 * 2 * CH, KB), c)
    out = lags(v.reshape(NTM, 12, 2, CH, KB), c, th, tl)
    return out.reshape(12, CH, 2 * BINS)


def solution(mesh):
    in_specs = (P("chan", "tm", None, None), P("chan", "tm"), P())
    out_specs = P("tm", "chan", None)
    return jax.shard_map(shards, mesh=mesh, in_specs=in_specs, out_specs=out_specs, check_vma=False)
```

```python
import functools
import math

import jax
import jax.numpy as jnp
from jax import lax
from jax.experimental import pallas as pl
from jax.experimental.pallas import tpu as pltpu
from jax.sharding import PartitionSpec as P

MESH = pl.DeviceIdType.MESH
ANY = pl.ANY
SRC = 3
NX = NY = 4
NTM = 8
CH = 32
SEG = 16
BINS = 1024
KB = BINS // NTM
ROWS = SRC * KB + CH
EARLY = 16
TOP = 32766.0
BIG = 56 * 1024 * 1024


def place():
    ch = lax.axis_index("chan")
    return ch // 8, lax.rem(ch // 2, 4), lax.rem(ch, 2), lax.axis_index("tm")


def device(y, x, zh, tm):
    return ((y * 4 + x) * 2 + zh, tm)


def up(v, d):
    return lax.rem(v + d, 4)


def greet(devices):
    bar = pltpu.get_barrier_semaphore()
    for d in devices:
        pl.semaphore_signal(bar, inc=1, device_id=d, device_id_type=MESH)
    pl.semaphore_wait(bar, len(devices))


def remote(src, dst, send, recv, where):
    copy = pltpu.make_async_remote_copy(
        src_ref=src, dst_ref=dst, send_sem=send, recv_sem=recv, device_id=where, device_id_type=MESH
    )
    copy.start()
    return copy


def front_body(plan, m, y_out, o_ref, r1, s1, r2, s2, rz, sh, yb, own_share, send, recv, local):
    y, x, zh, tm = place()
    tms = [lax.rem(tm + d, NTM) for d in range(1, NTM)]
    greet(
        [device(y, x, zh, t) for t in tms]
        + [device(y, up(x, d), zh, tm) for d in (1, 2, 3)]
        + [device(up(y, d), x, zh, tm) for d in (1, 2, 3)]
        + [device(y, x, 1 - zh, tm)]
    )
    ox = [lax.rem(plan[b] // 2, 4) for b in range(SRC)]
    oy = [plan[b] // 8 for b in range(SRC)]
    oz = [lax.rem(plan[b], 2) for b in range(SRC)]
    my_lanes = pl.ds(pl.multiple_of(tm * KB, KB), KB)
    my_rows = pl.ds(pl.multiple_of(tm * SEG, SEG), SEG)

    def bins_of(t):
        return pl.ds(pl.multiple_of(t * KB, KB), KB)

    def main(first, count, base):
        return [
            remote(
                m.at[pl.ds(first, count), :, :, bins_of(tms[d - 1])],
                y_out.at[pl.ds(first, count), :, my_rows, :],
                send.at[base + d],
                recv.at[base + d],
                device(y, x, zh, tms[d - 1]),
            )
            for d in range(1, NTM)
        ]

    def first_to(h, d):
        return (y, up(x, d)) if h == 0 else (up(y, d), x)

    def second_to(h, d):
        return first_to(1 - h, d)

    first_at, second_at = (x, y), (y, x)
    first_owner, second_owner = (ox, oy), (oy, ox)
    stage_1 = []
    for d in (1, 3, 2):
        for h in range(2):
            to = first_to(h, d)
            piece = pl.ds(16 * h + 4 * up(first_at[h], d), 4)
            stage_1.append(
                remote(
                    m.at[piece],
                    r1.at[h, first_at[h]],
                    send.at[3 * h + d],
                    recv.at[3 * h + d],
                    device(*to, zh, tm),
                )
            )
    own_1 = [
        pltpu.make_async_copy(
            m.at[pl.ds(16 * h + 4 * first_at[h], 4)], r1.at[h, first_at[h]], local.at[7 + h]
        )
        for h in range(2)
    ]
    for c in own_1:
        c.start()
    own_f = pltpu.make_async_copy(m.at[CH], sh.at[0], local.at[5])
    own_f.start()
    exchanged = main(0, EARLY, 73)
    own_m = pltpu.make_async_copy(
        m.at[pl.ds(0, CH), :, :, my_lanes], y_out.at[:, :, my_rows, :], local.at[1]
    )
    own_m.start()

    for c in own_1:
        c.wait()
    for c in stage_1:
        c.wait_recv()
    for h in range(2):
        for b in range(SRC):

            def pick(i, carry, h=h, b=b):
                s1[h, b, i] = r1[h, first_owner[h][b], i]
                return carry

            lax.fori_loop(0, 4, pick, 0)
    stage_2 = []
    for d in (1, 3, 2):
        for h in range(2):
            to = second_to(h, d)
            stage_2.append(
                remote(
                    s1.at[h, :, up(second_at[h], d)],
                    r2.at[h, second_at[h]],
                    send.at[6 + 3 * h + d],
                    recv.at[6 + 3 * h + d],
                    device(*to, zh, tm),
                )
            )
    own_2 = [
        pltpu.make_async_copy(
            s1.at[h, :, second_at[h]], r2.at[h, second_at[h]], local.at[2 * h]
        )
        for h in range(2)
    ]
    for c in own_2:
        c.start()
    for c in own_2:
        c.wait()
    for c in stage_2:
        c.wait_recv()
    for h in range(2):
        for b in range(SRC):
            s2[h, b] = r2[h, second_owner[h][b], b]
    stage_z = remote(s2.at[1 - zh], rz.at[zh], send.at[0], recv.at[0], device(y, x, 1 - zh, tm))
    own_z = pltpu.make_async_copy(s2.at[zh], rz.at[zh], local.at[3])
    own_z.start()
    own_z.wait()
    stage_z.wait_recv()
    own_f.wait()
    for b in range(SRC):
        sh[1 + b] = rz[oz[b], b]
    shares = [
        remote(
            sh.at[:, :, :, bins_of(tms[d - 1])],
            yb.at[:, :, my_rows, :],
            send.at[16 + d],
            recv.at[16 + d],
            device(y, x, zh, tms[d - 1]),
        )
        for d in range(1, NTM)
    ]
    own_s = pltpu.make_async_copy(sh.at[:, :, :, my_lanes], yb.at[:, :, my_rows, :], local.at[4])
    own_s.start()
    exchanged += main(EARLY, CH - EARLY, 24)
    own_s.wait()
    for c in shares:
        c.wait_recv()

    def turned(i, p):
        return yb[i, p].astype(jnp.float32).T

    for p in range(2):
        lanes = pl.ds(p * 128, 128)
        for b in range(SRC):
            own_share[pl.ds(b * KB, KB), lanes] = turned(1 + b, p).astype(jnp.bfloat16)
        own_share[pl.ds(SRC * KB, CH), lanes] = turned(0, p)[:CH].astype(jnp.bfloat16)

    cut = ROWS // 32 * 16
    me = y * 4 + x
    across = remote(
        own_share, o_ref.at[zh, me], send.at[32], recv.at[32], device(y, x, 1 - zh, tm)
    )
    own = pltpu.make_async_copy(own_share, o_ref.at[zh, me], local.at[6])
    own.start()
    started = []
    full, low, high = pl.ds(0, ROWS), pl.ds(0, cut), pl.ds(cut, ROWS - cut)

    class Half:
        def __init__(self, half):
            self.half = half
            ay, ax = half, 1 - half
            self.ap = device(up(y, ay), up(x, ax), zh, tm)
            self.am = device(up(y, 3 * ay), up(x, 3 * ax), zh, tm)
            self.bp = device(up(y, ax), up(x, ay), zh, tm)
            self.bm = device(up(y, 3 * ax), up(x, 3 * ay), zh, tm)
            self.a = x * ax + y * ay
            self.b = x * ay + y * ax
            self.base = 33 + 20 * half
            self.sent = {}
            self.passed = {}

        def put(self, b, a, part, k, where, source=None):
            slot = b * (4 - 3 * self.half) + a * (1 + 3 * self.half)
            ref = o_ref.at[self.half, slot, part]
            k = self.base + k
            copy = remote(ref if source is None else source, ref, send.at[k], recv.at[k], where)
            started.append(copy)
            return copy

        def at(self, r):
            return up(self.a, (0, 3, 1, 2)[r])

        def send_b(self, r, source=None):
            k = 4 + 4 * r
            self.sent[r] = (
                self.put(self.b, self.at(r), full, k, self.bp, source),
                self.put(self.b, self.at(r), full, k + 1, self.bm, source),
            )

        def start(self, source=None):
            self.a1 = self.put(self.b, self.a, full, 0, self.ap, source)
            self.a2 = self.put(self.b, self.a, full, 1, self.am, source)
            self.send_b(0, source)

        def first(self):
            self.a1.wait_recv()
            self.a3 = self.put(self.b, self.at(1), low, 2, self.ap)
            self.send_b(1)
            self.a2.wait_recv()
            self.a4 = self.put(self.b, self.at(2), high, 3, self.am)
            self.send_b(2)

        def second(self):
            self.a3.wait_recv()
            self.a4.wait_recv()
            self.send_b(3)

        def forward(self, r):
            k = 4 + 4 * r
            plus, minus = self.sent[r]
            plus.wait_recv()
            f1 = self.put(up(self.b, 3), self.at(r), low, k + 2, self.bp)
            minus.wait_recv()
            f2 = self.put(up(self.b, 1), self.at(r), high, k + 3, self.bm)
            self.passed[r] = (f1, f2)

    mine, other = Half(zh), Half(1 - zh)
    mine.start(own_share)
    mine.first()
    across.wait_recv()
    other.start()
    mine.forward(0)
    mine.second()
    other.first()
    mine.forward(1)
    other.forward(0)
    mine.forward(2)
    other.second()
    mine.forward(3)
    for r in (1, 2, 3):
        other.forward(r)
    for r in range(4):
        for h in (mine, other):
            for f in h.passed[r]:
                f.wait_recv()
    own.wait()
    own_m.wait()
    for c in exchanged:
        c.wait_recv()
    for c in stage_1 + stage_2 + [stage_z, across] + shares + exchanged + started:
        c.wait_send()


def front(plan, m):
    bf = jnp.bfloat16
    return pl.pallas_call(
        front_body,
        out_shape=(
            jax.ShapeDtypeStruct((CH, 2, NTM * SEG, KB), bf),
            jax.ShapeDtypeStruct((2, 16, ROWS, 256), bf),
        ),
        in_specs=[pl.BlockSpec(memory_space=pltpu.SMEM), pl.BlockSpec(memory_space=ANY)],
        out_specs=(pl.BlockSpec(memory_space=ANY), pl.BlockSpec(memory_space=ANY)),
        scratch_shapes=[
            pltpu.VMEM((2, 4, 4, 2, SEG, BINS), bf),
            pltpu.VMEM((2, SRC, 4, 2, SEG, BINS), bf),
            pltpu.VMEM((2, 4, SRC, 2, SEG, BINS), bf),
            pltpu.VMEM((2, SRC, 2, SEG, BINS), bf),
            pltpu.VMEM((2, SRC, 2, SEG, BINS), bf),
            pltpu.VMEM((1 + SRC, 2, SEG, BINS), bf),
            pltpu.VMEM((1 + SRC, 2, NTM * SEG, KB), bf),
            pltpu.VMEM((ROWS, 256), bf),
            pltpu.SemaphoreType.DMA((81,)),
            pltpu.SemaphoreType.DMA((81,)),
            pltpu.SemaphoreType.DMA((9,)),
        ],
        compiler_params=pltpu.CompilerParams(
            collective_id=0, has_side_effects=True, vmem_limit_bytes=BIG
        ),
    )(plan, m)


def correlate_body(plan, g_ref, y_ref, out_ref, scale_ref, sa, sq, ra, rq, ob):
    f32, bf = jnp.float32, jnp.bfloat16

    def widen(j, carry):
        zh, a, c = j // 16, lax.rem(j // 4, 4), lax.rem(j, 4)
        slot = c * (4 - 3 * zh) + a * (1 + 3 * zh)
        for b in range(SRC):
            rows = pl.ds(pl.multiple_of((b * CH + j) * KB, KB), KB)
            for p, part in enumerate((sa, sq)):
                lanes = pl.ds(p * 128, 128)
                part[rows, :] = g_ref[zh, slot, pl.ds(b * KB, KB), lanes].astype(f32)
        rows = pl.ds(pl.multiple_of(j * KB, KB), KB)
        for p, part in enumerate((ra, rq)):
            part[rows, :] = y_ref[j, p].astype(f32).T
        return carry

    lax.fori_loop(0, CH, widen, 0)

    def flags(block):
        return g_ref[lax.rem(block, 2), block // 2, pl.ds(SRC * KB, CH), pl.ds(0, 128)]

    fr = flags(lax.axis_index("chan"))
    fr = jnp.concatenate([fr, fr], axis=0)
    counts = []
    for b in range(SRC):
        fs = flags(plan[b])
        counts.append(
            lax.dot_general(fs, fr, (((1,), (1,)), ((), ())), preferred_element_type=f32)
        )
    inverse = 1.0 / jnp.maximum(jnp.concatenate(counts, axis=0), 1.0)

    def one(k, to):
        sources, channels = pl.ds(k, SRC * CH, stride=KB), pl.ds(k, CH, stride=KB)
        s = jnp.concatenate([sa[sources, :], sq[sources, :]], axis=1).astype(bf)
        a, q = ra[channels, :], rq[channels, :]
        real, imag = jnp.concatenate([a, q], axis=1), jnp.concatenate([q, -a], axis=1)
        both = jnp.concatenate([real, imag], axis=0).astype(bf)
        res = lax.dot_general(s, both, (((1,), (1,)), ((), ())), preferred_element_type=f32)
        res = res * inverse
        ob[pl.ds(to, SRC * CH, stride=KB), :] = jnp.concatenate([res, jnp.zeros_like(res)], axis=1)

    def some(i, carry):
        for u in range(8):
            one(i * 8 + u, i * 4 + u // 2 + u % 2 * (KB // 2))
        return carry

    lax.fori_loop(0, KB // 8, some, 0)

    def turn(t, carry):
        for i in range(12):
            s = t * 12 + i
            block = ob[pl.ds(pl.multiple_of(s * KB, KB), KB), pl.ds(0, 2 * CH)].T
            most = jnp.maximum(jnp.max(jnp.abs(block), axis=0, keepdims=True), 1e-30)
            code = jnp.round(block * (TOP / most)).astype(jnp.int32)
            out_ref[s] = code.astype(jnp.int16)
            scale_ref[t, pl.ds(i, 1), :] = most * (1.0 / TOP)
        return carry

    lax.fori_loop(0, NTM, turn, 0)


def correlate(plan, g, y):
    vmem = pl.BlockSpec(memory_space=pltpu.VMEM)
    return pl.pallas_call(
        correlate_body,
        out_shape=(
            jax.ShapeDtypeStruct((SRC * CH, 2 * CH, KB), jnp.int16),
            jax.ShapeDtypeStruct((NTM, 16, KB), jnp.float32),
        ),
        in_specs=[pl.BlockSpec(memory_space=pltpu.SMEM), vmem, vmem],
        out_specs=(vmem, vmem),
        scratch_shapes=[
            pltpu.VMEM((SRC * CH * KB, 128), jnp.float32),
            pltpu.VMEM((SRC * CH * KB, 128), jnp.float32),
            pltpu.VMEM((CH * KB, 128), jnp.float32),
            pltpu.VMEM((CH * KB, 128), jnp.float32),
            pltpu.VMEM((SRC * CH * KB, 128), jnp.float32),
        ],
        compiler_params=pltpu.CompilerParams(vmem_limit_bytes=BIG),
    )(plan, g, y)


def collect_body(
    x_ref, c_ref, c1, s1, c2, s2, v_ref, d_ref, th_ref, tl_ref, th, tl, send, recv, local
):
    y, x, zh, tm = place()
    tms = [lax.rem(tm + d, NTM) for d in range(1, NTM)]
    greet([device(y, x, zh, t) for t in tms])
    copies = []
    for d in range(1, NTM):
        t = tms[d - 1]
        for i, (src, dst) in enumerate(((x_ref, v_ref), (c_ref, d_ref))):
            copies.append(
                remote(src.at[t], dst.at[tm], send.at[i, d], recv.at[i, d], device(y, x, zh, t))
            )
    own = [
        pltpu.make_async_copy(src.at[tm], dst.at[tm], local.at[i])
        for i, (src, dst) in enumerate(((x_ref, v_ref), (c_ref, d_ref)))
    ]
    for c in own:
        c.start()

    def make(e1, carry):
        cos1 = jnp.broadcast_to(c1[pl.ds(e1, 1), :], (16, BINS))
        sin1 = jnp.broadcast_to(s1[pl.ds(e1, 1), :], (16, BINS))
        for parity in range(2):
            cos = cos1 * c2[parity] - sin1 * s2[parity]
            sin = -(sin1 * c2[parity] + cos1 * s2[parity])
            for p, value in enumerate((cos, sin)):
                high = value.astype(jnp.bfloat16)
                low = (value - high.astype(jnp.float32)).astype(jnp.bfloat16)
                th[parity, p, e1] = high
                tl[parity, p, e1] = low
        return carry

    lax.fori_loop(0, BINS // 32, make, 0)
    out = [
        pltpu.make_async_copy(th, th_ref, local.at[2]),
        pltpu.make_async_copy(tl, tl_ref, local.at[3]),
    ]
    for c in out:
        c.start()
    for c in own + copies + out:
        c.wait()


def collect(x, c, seeds):
    hbm, vmem = pl.BlockSpec(memory_space=ANY), pl.BlockSpec(memory_space=pltpu.VMEM)
    table = (2, 2, BINS // 32, 16, BINS)
    return pl.pallas_call(
        collect_body,
        out_shape=(
            jax.ShapeDtypeStruct(x.shape, x.dtype),
            jax.ShapeDtypeStruct(c.shape, c.dtype),
            jax.ShapeDtypeStruct(table, jnp.bfloat16),
            jax.ShapeDtypeStruct(table, jnp.bfloat16),
        ),
        in_specs=[hbm, hbm, vmem, vmem, vmem, vmem],
        out_specs=(hbm, hbm, hbm, hbm),
        scratch_shapes=[
            pltpu.VMEM(table, jnp.bfloat16),
            pltpu.VMEM(table, jnp.bfloat16),
            pltpu.SemaphoreType.DMA((2, NTM)),
            pltpu.SemaphoreType.DMA((2, NTM)),
            pltpu.SemaphoreType.DMA((4,)),
        ],
        compiler_params=pltpu.CompilerParams(
            collective_id=2, has_side_effects=True, vmem_limit_bytes=BIG
        ),
    )(x, c, *seeds)


def make_seeds():
    tau = lax.broadcasted_iota(jnp.int32, (1, BINS), 1)

    def pair(freq):
        angle = ((freq * tau) % (2 * BINS)).astype(jnp.float32) * (math.pi / BINS)
        return jnp.cos(angle), jnp.sin(angle)

    c1, s1 = pair(lax.broadcasted_iota(jnp.int32, (BINS // 32, 1), 0) * 32)
    row = lax.broadcasted_iota(jnp.int32, (32, 1), 0)
    c2, s2 = (
        (v / math.sqrt(BINS)).reshape(2, 16, BINS) for v in pair(row % 16 * 2 + row // 16)
    )
    return c1, s1, c2, s2


def lags_body(v_ref, c_ref, th_ref, tl_ref, out_ref, xh, xl):
    step = th_ref.shape[2]

    @pl.when(pl.program_id(0) == 0)
    def _():
        lane = lax.broadcasted_iota(jnp.int32, (CH, KB), 1)

        def split(s, carry):
            rows = pl.ds(pl.multiple_of(s * CH, CH), CH)
            for p in range(2):
                for j in range(NTM // 2):
                    a, b = (
                        v_ref[2 * j + i, s, p].astype(jnp.int32).astype(jnp.float32)
                        * c_ref[2 * j + i, pl.ds(s, 1), :]
                        for i in range(2)
                    )
                    even = jnp.where(lane < KB // 2, a, pltpu.roll(b, KB // 2, 1))
                    odd = jnp.where(lane < KB // 2, pltpu.roll(a, KB // 2, 1), b)
                    lanes = pl.ds(p * (BINS // 2) + j * KB, KB)
                    for parity, value in enumerate((even, odd)):
                        high = value.astype(jnp.bfloat16)
                        xh[parity, rows, lanes] = high
                        xl[parity, rows, lanes] = (value - high.astype(jnp.float32)).astype(
                            jnp.bfloat16
                        )
            return carry

        lax.fori_loop(0, 12, split, 0)

    def dot(a, b):
        return jnp.dot(a, b, preferred_element_type=jnp.float32)

    even, odd = (
        dot(xl[i], th_ref[i]) + dot(xh[i], tl_ref[i]) + dot(xh[i], th_ref[i]) for i in range(2)
    )
    at = pl.program_id(0) * step
    out_ref[:, pl.ds(pl.multiple_of(at, step), step)] = even - odd
    out_ref[:, pl.ds(pl.multiple_of(at + BINS, step), step)] = even + odd


def lags(v, c, th, tl):
    rows, step = 12 * CH, 256
    return pl.pallas_call(
        lags_body,
        grid=(BINS // step,),
        out_shape=jax.ShapeDtypeStruct((rows, 2 * BINS), jnp.float32),
        in_specs=[
            pl.BlockSpec((NTM, 12, 2, CH, KB), lambda g: (0, 0, 0, 0, 0)),
            pl.BlockSpec((NTM, 16, KB), lambda g: (0, 0, 0)),
            pl.BlockSpec((2, BINS, step), lambda g: (0, 0, g)),
            pl.BlockSpec((2, BINS, step), lambda g: (0, 0, g)),
        ],
        out_specs=pl.BlockSpec((rows, 2 * BINS), lambda g: (0, 0)),
        scratch_shapes=[
            pltpu.VMEM((2, rows, BINS), jnp.bfloat16),
            pltpu.VMEM((2, rows, BINS), jnp.bfloat16),
        ],
        compiler_params=pltpu.CompilerParams(vmem_limit_bytes=BIG),
    )(v, c, th, tl)


def shards(spectra, quality, plan):
    flags = quality.astype(jnp.bfloat16)
    masked = (spectra * flags[:, :, None, None]).transpose(0, 2, 1, 3)
    row = jnp.tile(jnp.pad(flags.T, ((0, 0), (0, KB - CH))), (1, NTM))
    m = jnp.concatenate([masked, jnp.broadcast_to(row, (1, 2, SEG, BINS))], axis=0)
    y, g = front(plan, m)
    x, c = correlate(plan, g, y)
    v, c, th, tl = collect(x.reshape(NTM, 12 * 2 * CH, KB), c, make_seeds())
    th, tl = (t.reshape(2, BINS, BINS) for t in (th, tl))
    out = lags(v.reshape(NTM, 12, 2, CH, KB), c, th, tl)
    return out.reshape(12, CH, 2 * BINS)


def solution(mesh):
    in_specs = (P("chan", "tm", None, None), P("chan", "tm"), P())
    out_specs = P("tm", "chan", None)
    return jax.shard_map(shards, mesh=mesh, in_specs=in_specs, out_specs=out_specs, check_vma=False)
```

```python
import functools
import math

import jax
import jax.numpy as jnp
from jax import lax
from jax.experimental import pallas as pl
from jax.experimental.pallas import tpu as pltpu
from jax.sharding import PartitionSpec as P
import numpy as np

MESH = pl.DeviceIdType.MESH
ANY = pl.ANY
SRC = 3
NX = NY = 4
NTM = 8
CH = 32
SEG = 16
BINS = 1024
KB = BINS // NTM
ROWS = SRC * KB + CH // 2
EARLY = 16
TOP = 32766.0
BIG = 56 * 1024 * 1024


def place():
    ch = lax.axis_index("chan")
    return ch // 8, lax.rem(ch // 2, 4), lax.rem(ch, 2), lax.axis_index("tm")


def device(y, x, zh, tm):
    return ((y * 4 + x) * 2 + zh, tm)


def up(v, d):
    return lax.rem(v + d, 4)


def greet(devices):
    bar = pltpu.get_barrier_semaphore()
    for d in devices:
        pl.semaphore_signal(bar, inc=1, device_id=d, device_id_type=MESH)
    pl.semaphore_wait(bar, len(devices))


def remote(src, dst, send, recv, where):
    copy = pltpu.make_async_remote_copy(
        src_ref=src, dst_ref=dst, send_sem=send, recv_sem=recv, device_id=where, device_id_type=MESH
    )
    copy.start()
    return copy


def front_body(plan, m, y_out, o_ref, r1, s1, r2, s2, fb, yb, own_share, send, recv, local):
    y, x, zh, tm = place()
    tms = [lax.rem(tm + d, NTM) for d in range(1, NTM)]
    greet(
        [device(y, x, zh, t) for t in tms]
        + [device(y, up(x, d), zh, tm) for d in (1, 2, 3)]
        + [device(up(y, d), x, zh, tm) for d in (1, 2, 3)]
        + [device(y, x, 1 - zh, t) for t in tms + [tm]]
    )
    ox = [lax.rem(plan[b] // 2, 4) for b in range(SRC)]
    oy = [plan[b] // 8 for b in range(SRC)]
    oz = [lax.rem(plan[b], 2) for b in range(SRC)]
    my_lanes = pl.ds(pl.multiple_of(tm * KB, KB), KB)
    my_rows = pl.ds(pl.multiple_of(tm * SEG, SEG), SEG)

    def bins_of(t):
        return pl.ds(pl.multiple_of(t * KB, KB), KB)

    def main(first, count, base):
        return [
            remote(
                m.at[pl.ds(first, count), :, :, bins_of(tms[d - 1])],
                y_out.at[pl.ds(first, count), :, my_rows, :],
                send.at[base + d],
                recv.at[base + d],
                device(y, x, zh, tms[d - 1]),
            )
            for d in range(1, NTM)
        ]

    def first_to(h, d):
        return (y, up(x, d)) if h == 0 else (up(y, d), x)

    def second_to(h, d):
        return first_to(1 - h, d)

    first_at, second_at = (x, y), (y, x)
    first_owner, second_owner = (ox, oy), (oy, ox)
    stage_1 = []
    for d in (1, 3, 2):
        for h in range(2):
            to = first_to(h, d)
            piece = pl.ds(16 * h + 4 * up(first_at[h], d), 4)
            stage_1.append(
                remote(
                    m.at[piece],
                    r1.at[h, first_at[h]],
                    send.at[3 * h + d],
                    recv.at[3 * h + d],
                    device(*to, zh, tm),
                )
            )
    own_1 = [
        pltpu.make_async_copy(
            m.at[pl.ds(16 * h + 4 * first_at[h], 4)], r1.at[h, first_at[h]], local.at[7 + h]
        )
        for h in range(2)
    ]
    for c in own_1:
        c.start()
    flags = [
        remote(
            m.at[CH, 0, :, bins_of(t)],
            fb.at[my_rows, :],
            send.at[24 + d],
            recv.at[24 + d],
            device(y, x, zh, t),
        )
        for d, t in enumerate(tms, 1)
    ]
    own_f = pltpu.make_async_copy(m.at[CH, 0, :, my_lanes], fb.at[my_rows, :], local.at[5])
    own_f.start()
    exchanged = main(0, EARLY, 73)
    own_m = pltpu.make_async_copy(
        m.at[pl.ds(0, CH), :, :, my_lanes], y_out.at[:, :, my_rows, :], local.at[1]
    )
    own_m.start()

    for c in own_1:
        c.wait()
    for c in stage_1:
        c.wait_recv()
    for h in range(2):
        for b in range(SRC):

            def pick(i, carry, h=h, b=b):
                s1[h, b, i] = r1[h, first_owner[h][b], i]
                return carry

            lax.fori_loop(0, 4, pick, 0)
    stage_2 = []
    for d in (1, 3, 2):
        for h in range(2):
            to = second_to(h, d)
            stage_2.append(
                remote(
                    s1.at[h, :, up(second_at[h], d)],
                    r2.at[h, second_at[h]],
                    send.at[6 + 3 * h + d],
                    recv.at[6 + 3 * h + d],
                    device(*to, zh, tm),
                )
            )
    own_2 = [
        pltpu.make_async_copy(
            s1.at[h, :, second_at[h]], r2.at[h, second_at[h]], local.at[2 * h]
        )
        for h in range(2)
    ]
    for c in own_2:
        c.start()
    for c in own_2:
        c.wait()
    for c in stage_2:
        c.wait_recv()
    for h in range(2):
        for b in range(SRC):
            s2[h, b] = r2[h, second_owner[h][b], b]
    shares = []
    for other in range(2):
        half = zh + other * (1 - 2 * zh)
        for d in range(1 - other, NTM):
            t = lax.rem(tm + d, NTM)
            k = 81 + 8 * other + d
            shares.append(
                remote(
                    s2.at[half, :, :, :, bins_of(t)],
                    yb.at[zh, :, :, my_rows, :],
                    send.at[k],
                    recv.at[k],
                    device(y, x, half, t),
                )
            )
    own_s = pltpu.make_async_copy(
        s2.at[zh, :, :, :, my_lanes], yb.at[zh, :, :, my_rows, :], local.at[4]
    )
    own_s.start()
    exchanged += main(EARLY, CH - EARLY, 15)
    own_s.wait()
    own_f.wait()
    for c in flags + shares:
        c.wait_recv()

    for p in range(2):
        lanes = pl.ds(p * 128, 128)
        for b in range(SRC):
            part = yb[oz[b], b, p].astype(jnp.float32).T
            own_share[pl.ds(b * KB, KB), lanes] = part.astype(jnp.bfloat16)
    part = fb[...].astype(jnp.float32).T.astype(jnp.bfloat16)
    for i in range(2):
        own_share[pl.ds(SRC * KB, CH // 2), pl.ds(i * 128, 128)] = part[i * 16 : i * 16 + 16]

    cut = ROWS // 32 * 16
    me = y * 4 + x
    across = remote(
        own_share, o_ref.at[zh, me], send.at[32], recv.at[32], device(y, x, 1 - zh, tm)
    )
    own = pltpu.make_async_copy(own_share, o_ref.at[zh, me], local.at[6])
    own.start()
    started = []
    full, low, high = pl.ds(0, ROWS), pl.ds(0, cut), pl.ds(cut, ROWS - cut)

    class Half:
        def __init__(self, half):
            self.half = half
            ay, ax = half, 1 - half
            self.ap = device(up(y, ay), up(x, ax), zh, tm)
            self.am = device(up(y, 3 * ay), up(x, 3 * ax), zh, tm)
            self.bp = device(up(y, ax), up(x, ay), zh, tm)
            self.bm = device(up(y, 3 * ax), up(x, 3 * ay), zh, tm)
            self.a = x * ax + y * ay
            self.b = x * ay + y * ax
            self.base = 33 + 20 * half
            self.sent = {}
            self.passed = {}

        def put(self, b, a, part, k, where, source=None):
            slot = b * (4 - 3 * self.half) + a * (1 + 3 * self.half)
            ref = o_ref.at[self.half, slot, part]
            k = self.base + k
            copy = remote(ref if source is None else source, ref, send.at[k], recv.at[k], where)
            started.append(copy)
            return copy

        def at(self, r):
            return up(self.a, (0, 3, 1, 2)[r])

        def send_b(self, r, source=None):
            k = 4 + 4 * r
            self.sent[r] = (
                self.put(self.b, self.at(r), full, k, self.bp, source),
                self.put(self.b, self.at(r), full, k + 1, self.bm, source),
            )

        def start(self, source=None):
            self.a1 = self.put(self.b, self.a, full, 0, self.ap, source)
            self.a2 = self.put(self.b, self.a, full, 1, self.am, source)
            self.send_b(0, source)

        def first(self):
            self.a1.wait_recv()
            self.a3 = self.put(self.b, self.at(1), low, 2, self.ap)
            self.send_b(1)
            self.a2.wait_recv()
            self.a4 = self.put(self.b, self.at(2), high, 3, self.am)
            self.send_b(2)

        def second(self):
            self.a3.wait_recv()
            self.a4.wait_recv()
            self.send_b(3)

        def forward(self, r):
            k = 4 + 4 * r
            plus, minus = self.sent[r]
            plus.wait_recv()
            f1 = self.put(up(self.b, 3), self.at(r), low, k + 2, self.bp)
            minus.wait_recv()
            f2 = self.put(up(self.b, 1), self.at(r), high, k + 3, self.bm)
            self.passed[r] = (f1, f2)

    mine, other = Half(zh), Half(1 - zh)
    mine.start(own_share)
    mine.first()
    across.wait_recv()
    other.start()
    mine.forward(0)
    mine.second()
    other.first()
    mine.forward(1)
    other.forward(0)
    mine.forward(2)
    other.second()
    mine.forward(3)
    for r in (1, 2, 3):
        other.forward(r)
    for r in range(4):
        for h in (mine, other):
            for f in h.passed[r]:
                f.wait_recv()
    own.wait()
    own_m.wait()
    for c in exchanged:
        c.wait_recv()
    for c in stage_1 + stage_2 + [across] + flags + shares + exchanged + started:
        c.wait_send()


def front(plan, m):
    bf = jnp.bfloat16
    return pl.pallas_call(
        front_body,
        out_shape=(
            jax.ShapeDtypeStruct((CH, 2, NTM * SEG, KB), bf),
            jax.ShapeDtypeStruct((2, 16, ROWS, 256), bf),
        ),
        in_specs=[pl.BlockSpec(memory_space=pltpu.SMEM), pl.BlockSpec(memory_space=ANY)],
        out_specs=(pl.BlockSpec(memory_space=ANY), pl.BlockSpec(memory_space=ANY)),
        scratch_shapes=[
            pltpu.VMEM((2, 4, 4, 2, SEG, BINS), bf),
            pltpu.VMEM((2, SRC, 4, 2, SEG, BINS), bf),
            pltpu.VMEM((2, 4, SRC, 2, SEG, BINS), bf),
            pltpu.VMEM((2, SRC, 2, SEG, BINS), bf),
            pltpu.VMEM((NTM * SEG, KB), bf),
            pltpu.VMEM((2, SRC, 2, NTM * SEG, KB), bf),
            pltpu.VMEM((ROWS, 256), bf),
            pltpu.SemaphoreType.DMA((97,)),
            pltpu.SemaphoreType.DMA((97,)),
            pltpu.SemaphoreType.DMA((9,)),
        ],
        compiler_params=pltpu.CompilerParams(
            collective_id=0, has_side_effects=True, vmem_limit_bytes=BIG
        ),
    )(plan, m)


def correlate_body(plan, g_ref, y_ref, out_ref, scale_ref, sa, sq, ra, rq, ob):
    f32, bf = jnp.float32, jnp.bfloat16

    def widen(j, carry):
        zh, a, c = j // 16, lax.rem(j // 4, 4), lax.rem(j, 4)
        slot = c * (4 - 3 * zh) + a * (1 + 3 * zh)
        for b in range(SRC):
            rows = pl.ds(pl.multiple_of((b * CH + j) * KB, KB), KB)
            for p, part in enumerate((sa, sq)):
                lanes = pl.ds(p * 128, 128)
                part[rows, :] = g_ref[zh, slot, pl.ds(b * KB, KB), lanes].astype(f32)
        rows = pl.ds(pl.multiple_of(j * KB, KB), KB)
        for p, part in enumerate((ra, rq)):
            part[rows, :] = y_ref[j, p].astype(f32).T
        return carry

    lax.fori_loop(0, CH, widen, 0)

    def flags(block):
        rows = pl.ds(SRC * KB, CH // 2)
        return jnp.concatenate(
            [g_ref[lax.rem(block, 2), block // 2, rows, pl.ds(i * 128, 128)] for i in range(2)]
        )

    fr = flags(lax.axis_index("chan"))
    fr = jnp.concatenate([fr, fr], axis=0)
    counts = []
    for b in range(SRC):
        fs = flags(plan[b])
        counts.append(
            lax.dot_general(fs, fr, (((1,), (1,)), ((), ())), preferred_element_type=f32)
        )
    inverse = 1.0 / jnp.maximum(jnp.concatenate(counts, axis=0), 1.0)

    def one(k, to):
        sources, channels = pl.ds(k, SRC * CH, stride=KB), pl.ds(k, CH, stride=KB)
        s = jnp.concatenate([sa[sources, :], sq[sources, :]], axis=1).astype(bf)
        a, q = ra[channels, :], rq[channels, :]
        real, imag = jnp.concatenate([a, q], axis=1), jnp.concatenate([q, -a], axis=1)
        both = jnp.concatenate([real, imag], axis=0).astype(bf)
        res = lax.dot_general(s, both, (((1,), (1,)), ((), ())), preferred_element_type=f32)
        res = res * inverse
        ob[pl.ds(to, SRC * CH, stride=KB), :] = jnp.concatenate([res, jnp.zeros_like(res)], axis=1)

    def some(i, carry):
        for u in range(8):
            one(i * 8 + u, i * 4 + u // 2 + u % 2 * (KB // 2))
        return carry

    lax.fori_loop(0, KB // 8, some, 0)

    def turn(t, carry):
        for i in range(12):
            s = t * 12 + i
            block = ob[pl.ds(pl.multiple_of(s * KB, KB), KB), pl.ds(0, 2 * CH)].T
            most = jnp.maximum(jnp.max(jnp.abs(block), axis=0, keepdims=True), 1e-30)
            code = jnp.round(block * (TOP / most)).astype(jnp.int32)
            out_ref[s] = code.astype(jnp.int16)
            scale_ref[t, pl.ds(i, 1), :] = most * (1.0 / TOP)
        return carry

    lax.fori_loop(0, NTM, turn, 0)


def correlate(plan, g, y):
    vmem = pl.BlockSpec(memory_space=pltpu.VMEM)
    return pl.pallas_call(
        correlate_body,
        out_shape=(
            jax.ShapeDtypeStruct((SRC * CH, 2 * CH, KB), jnp.int16),
            jax.ShapeDtypeStruct((NTM, 16, KB), jnp.float32),
        ),
        in_specs=[pl.BlockSpec(memory_space=pltpu.SMEM), vmem, vmem],
        out_specs=(vmem, vmem),
        scratch_shapes=[
            pltpu.VMEM((SRC * CH * KB, 128), jnp.float32),
            pltpu.VMEM((SRC * CH * KB, 128), jnp.float32),
            pltpu.VMEM((CH * KB, 128), jnp.float32),
            pltpu.VMEM((CH * KB, 128), jnp.float32),
            pltpu.VMEM((SRC * CH * KB, 128), jnp.float32),
        ],
        compiler_params=pltpu.CompilerParams(vmem_limit_bytes=BIG),
    )(plan, g, y)


def collect_body(
    x_ref, c_ref, c1, s1, c2, s2, v_ref, d_ref, th_ref, tl_ref, th, tl, send, recv, local
):
    y, x, zh, tm = place()
    tms = [lax.rem(tm + d, NTM) for d in range(1, NTM)]
    greet([device(y, x, zh, t) for t in tms])
    copies = []
    for d in range(1, NTM):
        t = tms[d - 1]
        for i, (src, dst) in enumerate(((x_ref, v_ref), (c_ref, d_ref))):
            copies.append(
                remote(src.at[t], dst.at[tm], send.at[i, d], recv.at[i, d], device(y, x, zh, t))
            )
    own = [
        pltpu.make_async_copy(src.at[tm], dst.at[tm], local.at[i])
        for i, (src, dst) in enumerate(((x_ref, v_ref), (c_ref, d_ref)))
    ]
    for c in own:
        c.start()

    def make(e1, carry):
        cos1 = jnp.broadcast_to(c1[pl.ds(e1, 1), :], (16, BINS))
        sin1 = jnp.broadcast_to(s1[pl.ds(e1, 1), :], (16, BINS))
        for parity in range(2):
            cos = cos1 * c2[parity] - sin1 * s2[parity]
            sin = -(sin1 * c2[parity] + cos1 * s2[parity])
            for p, value in enumerate((cos, sin)):
                high = value.astype(jnp.bfloat16)
                low = (value - high.astype(jnp.float32)).astype(jnp.bfloat16)
                th[parity, p, e1] = high
                tl[parity, p, e1] = low
        return carry

    lax.fori_loop(0, BINS // 32, make, 0)
    out = [
        pltpu.make_async_copy(th, th_ref, local.at[2]),
        pltpu.make_async_copy(tl, tl_ref, local.at[3]),
    ]
    for c in out:
        c.start()
    for c in own + copies + out:
        c.wait()


def collect(x, c, seeds):
    hbm, vmem = pl.BlockSpec(memory_space=ANY), pl.BlockSpec(memory_space=pltpu.VMEM)
    table = (2, 2, BINS // 32, 16, BINS)
    return pl.pallas_call(
        collect_body,
        out_shape=(
            jax.ShapeDtypeStruct(x.shape, x.dtype),
            jax.ShapeDtypeStruct(c.shape, c.dtype),
            jax.ShapeDtypeStruct(table, jnp.bfloat16),
            jax.ShapeDtypeStruct(table, jnp.bfloat16),
        ),
        in_specs=[hbm, hbm, vmem, vmem, vmem, vmem],
        out_specs=(hbm, hbm, hbm, hbm),
        scratch_shapes=[
            pltpu.VMEM(table, jnp.bfloat16),
            pltpu.VMEM(table, jnp.bfloat16),
            pltpu.SemaphoreType.DMA((2, NTM)),
            pltpu.SemaphoreType.DMA((2, NTM)),
            pltpu.SemaphoreType.DMA((4,)),
        ],
        compiler_params=pltpu.CompilerParams(
            collective_id=2, has_side_effects=True, vmem_limit_bytes=BIG
        ),
    )(x, c, *seeds)


def make_seeds():
    tau = np.arange(BINS)

    def pair(freq):
        angle = (np.multiply.outer(freq, tau) % (2 * BINS)) * (math.pi / BINS)
        return np.cos(angle), np.sin(angle)

    c1, s1 = pair(np.arange(BINS // 32) * 32)
    c2, s2 = pair(np.add.outer(np.arange(2), 2 * np.arange(16)))
    scale = 1.0 / math.sqrt(BINS)
    return [jnp.asarray(v, jnp.float32) for v in (c1, s1, c2 * scale, s2 * scale)]


def lags_body(v_ref, c_ref, th_ref, tl_ref, out_ref, xh, xl):
    step = th_ref.shape[2]

    @pl.when(pl.program_id(0) == 0)
    def _():
        lane = lax.broadcasted_iota(jnp.int32, (CH, KB), 1)

        def split(s, carry):
            rows = pl.ds(pl.multiple_of(s * CH, CH), CH)
            for p in range(2):
                for j in range(NTM // 2):
                    a, b = (
                        v_ref[2 * j + i, s, p].astype(jnp.int32).astype(jnp.float32)
                        * c_ref[2 * j + i, pl.ds(s, 1), :]
                        for i in range(2)
                    )
                    even = jnp.where(lane < KB // 2, a, pltpu.roll(b, KB // 2, 1))
                    odd = jnp.where(lane < KB // 2, pltpu.roll(a, KB // 2, 1), b)
                    lanes = pl.ds(p * (BINS // 2) + j * KB, KB)
                    for parity, value in enumerate((even, odd)):
                        high = value.astype(jnp.bfloat16)
                        xh[parity, rows, lanes] = high
                        xl[parity, rows, lanes] = (value - high.astype(jnp.float32)).astype(
                            jnp.bfloat16
                        )
            return carry

        lax.fori_loop(0, 12, split, 0)

    def dot(a, b):
        return jnp.dot(a, b, preferred_element_type=jnp.float32)

    even, odd = (
        dot(xl[i], th_ref[i]) + dot(xh[i], tl_ref[i]) + dot(xh[i], th_ref[i]) for i in range(2)
    )
    at = pl.program_id(0) * step
    out_ref[:, pl.ds(pl.multiple_of(at, step), step)] = even - odd
    out_ref[:, pl.ds(pl.multiple_of(at + BINS, step), step)] = even + odd


def lags(v, c, th, tl):
    rows, step = 12 * CH, 256
    return pl.pallas_call(
        lags_body,
        grid=(BINS // step,),
        out_shape=jax.ShapeDtypeStruct((rows, 2 * BINS), jnp.float32),
        in_specs=[
            pl.BlockSpec((NTM, 12, 2, CH, KB), lambda g: (0, 0, 0, 0, 0)),
            pl.BlockSpec((NTM, 16, KB), lambda g: (0, 0, 0)),
            pl.BlockSpec((2, BINS, step), lambda g: (0, 0, g)),
            pl.BlockSpec((2, BINS, step), lambda g: (0, 0, g)),
        ],
        out_specs=pl.BlockSpec((rows, 2 * BINS), lambda g: (0, 0)),
        scratch_shapes=[
            pltpu.VMEM((2, rows, BINS), jnp.bfloat16),
            pltpu.VMEM((2, rows, BINS), jnp.bfloat16),
        ],
        compiler_params=pltpu.CompilerParams(vmem_limit_bytes=BIG),
    )(v, c, th, tl)


def shards(spectra, quality, plan):
    flags = quality.astype(jnp.bfloat16)
    masked = (spectra * flags[:, :, None, None]).transpose(0, 2, 1, 3)
    row = jnp.tile(jnp.pad(flags.T, ((0, 0), (0, KB - CH))), (1, NTM))
    m = jnp.concatenate([masked, jnp.broadcast_to(row, (1, 2, SEG, BINS))], axis=0)
    y, g = front(plan, m)
    x, c = correlate(plan, g, y)
    v, c, th, tl = collect(x.reshape(NTM, 12 * 2 * CH, KB), c, make_seeds())
    th, tl = (t.reshape(2, BINS, BINS) for t in (th, tl))
    out = lags(v.reshape(NTM, 12, 2, CH, KB), c, th, tl)
    return out.reshape(12, CH, 2 * BINS)


def solution(mesh):
    in_specs = (P("chan", "tm", None, None), P("chan", "tm"), P())
    out_specs = P("tm", "chan", None)
    return jax.shard_map(shards, mesh=mesh, in_specs=in_specs, out_specs=out_specs, check_vma=False)
```

```python
import functools
import math

import jax
import jax.numpy as jnp
from jax import lax
from jax.experimental import pallas as pl
from jax.experimental.pallas import tpu as pltpu
from jax.sharding import PartitionSpec as P
import numpy as np

MESH = pl.DeviceIdType.MESH
ANY = pl.ANY
SRC = 3
NX = NY = 4
NTM = 8
CH = 32
SEG = 16
BINS = 1024
KB = BINS // NTM
ROWS = SRC * KB + CH // 2
HALF = 48
EARLY = 16
TOP = 32766.0
BIG = 56 * 1024 * 1024


def place():
    ch = lax.axis_index("chan")
    return ch // 8, lax.rem(ch // 2, 4), lax.rem(ch, 2), lax.axis_index("tm")


def device(y, x, zh, tm):
    return ((y * 4 + x) * 2 + zh, tm)


def up(v, d):
    return lax.rem(v + d, 4)


def greet(devices):
    bar = pltpu.get_barrier_semaphore()
    for d in devices:
        pl.semaphore_signal(bar, inc=1, device_id=d, device_id_type=MESH)
    pl.semaphore_wait(bar, len(devices))


def remote(src, dst, send, recv, where):
    copy = pltpu.make_async_remote_copy(
        src_ref=src, dst_ref=dst, send_sem=send, recv_sem=recv, device_id=where, device_id_type=MESH
    )
    copy.start()
    return copy


def stack_body(
    plan, m, c1, n1, c2, n2, v_ref, d_ref, inv_ref, th_ref, tl_ref,
    r1, s1, r2, s2, fb, yb, own_share, y_out, o_ref, sa, sq, ra, rq, ob, inv, codes, scales, th, tl,
    send, recv, local, code_send, code_recv, code_local,
):
    f32, bf = jnp.float32, jnp.bfloat16
    y, x, zh, tm = place()
    tms = [lax.rem(tm + d, NTM) for d in range(1, NTM)]
    greet(
        [device(y, x, zh, t) for t in tms]
        + [device(y, up(x, d), zh, tm) for d in (1, 2, 3)]
        + [device(up(y, d), x, zh, tm) for d in (1, 2, 3)]
        + [device(y, x, 1 - zh, t) for t in tms + [tm]]
    )
    ox = [lax.rem(plan[b] // 2, 4) for b in range(SRC)]
    oy = [plan[b] // 8 for b in range(SRC)]
    oz = [lax.rem(plan[b], 2) for b in range(SRC)]
    my_lanes = pl.ds(pl.multiple_of(tm * KB, KB), KB)
    my_rows = pl.ds(pl.multiple_of(tm * SEG, SEG), SEG)

    def bins_of(t):
        return pl.ds(pl.multiple_of(t * KB, KB), KB)

    def main(first, count, base):
        return [
            remote(
                m.at[pl.ds(first, count), :, :, bins_of(tms[d - 1])],
                y_out.at[pl.ds(first, count), :, my_rows, :],
                send.at[base + d],
                recv.at[base + d],
                device(y, x, zh, tms[d - 1]),
            )
            for d in range(1, NTM)
        ]

    def first_to(h, d):
        return (y, up(x, d)) if h == 0 else (up(y, d), x)

    def second_to(h, d):
        return first_to(1 - h, d)

    first_at, second_at = (x, y), (y, x)
    first_owner, second_owner = (ox, oy), (oy, ox)
    stage_1 = []
    for d in (1, 3, 2):
        for h in range(2):
            to = first_to(h, d)
            piece = pl.ds(16 * h + 4 * up(first_at[h], d), 4)
            stage_1.append(
                remote(
                    m.at[piece],
                    r1.at[h, first_at[h]],
                    send.at[3 * h + d],
                    recv.at[3 * h + d],
                    device(*to, zh, tm),
                )
            )
    own_1 = [
        pltpu.make_async_copy(
            m.at[pl.ds(16 * h + 4 * first_at[h], 4)], r1.at[h, first_at[h]], local.at[7 + h]
        )
        for h in range(2)
    ]
    for c in own_1:
        c.start()
    flags = [
        remote(
            m.at[CH, 0, :, bins_of(t)],
            fb.at[my_rows, :],
            send.at[24 + d],
            recv.at[24 + d],
            device(y, x, zh, t),
        )
        for d, t in enumerate(tms, 1)
    ]
    own_f = pltpu.make_async_copy(m.at[CH, 0, :, my_lanes], fb.at[my_rows, :], local.at[5])
    own_f.start()
    exchanged = main(0, EARLY, 73)
    own_m = pltpu.make_async_copy(
        m.at[pl.ds(0, CH), :, :, my_lanes], y_out.at[:, :, my_rows, :], local.at[1]
    )
    own_m.start()

    def make(e1, carry):
        cos1 = jnp.broadcast_to(c1[pl.ds(e1, 1), :], (16, BINS))
        sin1 = jnp.broadcast_to(n1[pl.ds(e1, 1), :], (16, BINS))
        for parity in range(2):
            cos = cos1 * c2[parity] - sin1 * n2[parity]
            sin = -(sin1 * c2[parity] + cos1 * n2[parity])
            for p, value in enumerate((cos, sin)):
                high = value.astype(bf)
                th[parity, p, e1] = high
                tl[parity, p, e1] = (value - high.astype(f32)).astype(bf)
        return carry

    lax.fori_loop(0, BINS // 32, make, 0)
    tables = [
        pltpu.make_async_copy(th, th_ref, local.at[9]),
        pltpu.make_async_copy(tl, tl_ref, local.at[10]),
    ]
    for c in tables:
        c.start()
    scales[...] = jnp.zeros_like(scales)

    for c in own_1:
        c.wait()
    for c in stage_1:
        c.wait_recv()
    for h in range(2):
        for b in range(SRC):

            def pick(i, carry, h=h, b=b):
                s1[h, b, i] = r1[h, first_owner[h][b], i]
                return carry

            lax.fori_loop(0, 4, pick, 0)
    stage_2 = []
    for d in (1, 3, 2):
        for h in range(2):
            to = second_to(h, d)
            stage_2.append(
                remote(
                    s1.at[h, :, up(second_at[h], d)],
                    r2.at[h, second_at[h]],
                    send.at[6 + 3 * h + d],
                    recv.at[6 + 3 * h + d],
                    device(*to, zh, tm),
                )
            )
    own_2 = [
        pltpu.make_async_copy(
            s1.at[h, :, second_at[h]], r2.at[h, second_at[h]], local.at[2 * h]
        )
        for h in range(2)
    ]
    for c in own_2:
        c.start()
    for c in own_2:
        c.wait()
    for c in stage_2:
        c.wait_recv()
    for h in range(2):
        for b in range(SRC):
            s2[h, b] = r2[h, second_owner[h][b], b]
    shares = []
    for other in range(2):
        half = zh + other * (1 - 2 * zh)
        for d in range(1 - other, NTM):
            t = lax.rem(tm + d, NTM)
            k = 81 + 8 * other + d
            shares.append(
                remote(
                    s2.at[half, :, :, :, bins_of(t)],
                    yb.at[zh, :, :, my_rows, :],
                    send.at[k],
                    recv.at[k],
                    device(y, x, half, t),
                )
            )
    own_s = pltpu.make_async_copy(
        s2.at[zh, :, :, :, my_lanes], yb.at[zh, :, :, my_rows, :], local.at[4]
    )
    own_s.start()
    exchanged += main(EARLY, CH - EARLY, 15)
    own_s.wait()
    own_f.wait()
    for c in flags + shares:
        c.wait_recv()

    for p in range(2):
        lanes = pl.ds(p * 128, 128)
        for b in range(SRC):
            part = yb[oz[b], b, p].astype(jnp.float32).T
            own_share[pl.ds(b * KB, KB), lanes] = part.astype(jnp.bfloat16)
    part = fb[...].astype(jnp.float32).T.astype(jnp.bfloat16)
    for i in range(2):
        own_share[pl.ds(SRC * KB, CH // 2), pl.ds(i * 128, 128)] = part[i * 16 : i * 16 + 16]

    cut = ROWS // 32 * 16
    me = y * 4 + x
    across = remote(
        own_share, o_ref.at[zh, me], send.at[32], recv.at[32], device(y, x, 1 - zh, tm)
    )
    own = pltpu.make_async_copy(own_share, o_ref.at[zh, me], local.at[6])
    own.start()
    started = []
    full, low, high = pl.ds(0, ROWS), pl.ds(0, cut), pl.ds(cut, ROWS - cut)

    class Half:
        def __init__(self, half):
            self.half = half
            ay, ax = half, 1 - half
            self.ap = device(up(y, ay), up(x, ax), zh, tm)
            self.am = device(up(y, 3 * ay), up(x, 3 * ax), zh, tm)
            self.bp = device(up(y, ax), up(x, ay), zh, tm)
            self.bm = device(up(y, 3 * ax), up(x, 3 * ay), zh, tm)
            self.a = x * ax + y * ay
            self.b = x * ay + y * ax
            self.base = 33 + 20 * half
            self.sent = {}
            self.passed = {}

        def put(self, b, a, part, k, where, source=None):
            slot = b * (4 - 3 * self.half) + a * (1 + 3 * self.half)
            ref = o_ref.at[self.half, slot, part]
            k = self.base + k
            copy = remote(ref if source is None else source, ref, send.at[k], recv.at[k], where)
            started.append(copy)
            return copy

        def at(self, r):
            return up(self.a, (0, 3, 1, 2)[r])

        def send_b(self, r, source=None):
            k = 4 + 4 * r
            self.sent[r] = (
                self.put(self.b, self.at(r), full, k, self.bp, source),
                self.put(self.b, self.at(r), full, k + 1, self.bm, source),
            )

        def start(self, source=None):
            self.a1 = self.put(self.b, self.a, full, 0, self.ap, source)
            self.a2 = self.put(self.b, self.a, full, 1, self.am, source)
            self.send_b(0, source)

        def first(self):
            self.a1.wait_recv()
            self.a3 = self.put(self.b, self.at(1), low, 2, self.ap)
            self.send_b(1)
            self.a2.wait_recv()
            self.a4 = self.put(self.b, self.at(2), high, 3, self.am)
            self.send_b(2)

        def second(self):
            self.a3.wait_recv()
            self.a4.wait_recv()
            self.send_b(3)

        def forward(self, r):
            k = 4 + 4 * r
            plus, minus = self.sent[r]
            plus.wait_recv()
            f1 = self.put(up(self.b, 3), self.at(r), low, k + 2, self.bp)
            minus.wait_recv()
            f2 = self.put(up(self.b, 1), self.at(r), high, k + 3, self.bm)
            self.passed[r] = (f1, f2)

    mine, other = Half(zh), Half(1 - zh)

    def landed(r):
        for h in (mine, other):
            for f in h.passed[r]:
                f.wait_recv()

    def group(g, between):
        def coords(q):
            blk, h, ri = q // 4, lax.rem(q // 2, 2), lax.rem(q, 2)
            return blk, h, up(x + h * (y - x), 3 * ri if g == 0 else 1 + ri)

        def widen(q, carry):
            blk, h, a = coords(q)
            for bb in range(4):
                rows = pl.ds(pl.multiple_of((q * 4 + bb) * KB, KB), KB)
                slot = bb * (4 - 3 * h) + a * (1 + 3 * h)
                tile = pl.ds(pl.multiple_of(blk * KB, KB), KB)
                for p, part in enumerate((sa, sq)):
                    part[rows, :] = o_ref[h, slot, tile, pl.ds(p * 128, 128)].astype(f32)
            return carry

        lax.fori_loop(0, 12, widen, 0)
        between()

        def one(k, to):
            sources, channels = pl.ds(k, HALF, stride=KB), pl.ds(k, CH, stride=KB)
            s = jnp.concatenate([sa[sources, :], sq[sources, :]], axis=1).astype(bf)
            a, q = ra[channels, :], rq[channels, :]
            real, imag = jnp.concatenate([a, q], axis=1), jnp.concatenate([q, -a], axis=1)
            both = jnp.concatenate([real, imag], axis=0).astype(bf)
            res = lax.dot_general(s, both, (((1,), (1,)), ((), ())), preferred_element_type=f32)
            ob[pl.ds(to, HALF, stride=KB), :] = jnp.concatenate([res, jnp.zeros_like(res)], axis=1)

        def some(i, carry):
            for t in range(8):
                one(i * 8 + t, i * 4 + t // 2 + t % 2 * (KB // 2))
            return carry

        lax.fori_loop(0, KB // 8, some, 0)

        def turn(q, carry):
            blk, h, a = coords(q)
            u = 8 * blk + 4 * h + a
            to, at = u // 3, lax.rem(u, 3)
            for bb in range(4):
                block = ob[pl.ds(pl.multiple_of((q * 4 + bb) * KB, KB), KB), :]
                most = jnp.maximum(jnp.max(jnp.abs(block), axis=0, keepdims=True), 1e-30)
                code = jnp.round(block * (TOP / most)).T[: 2 * CH]
                codes[u, bb] = code.astype(jnp.int32).astype(jnp.int16)
                scales[to, pl.ds(at * 4 + bb, 1), :] = most * (1.0 / TOP)

            @pl.when(to != tm)
            def _():
                code_to(u, to, at).start()

            @pl.when(to == tm)
            def _():
                code_here(u, at).start()

            return carry

        lax.fori_loop(0, 12, turn, 0)

    def code_to(u, to, at):
        return pltpu.make_async_remote_copy(
            src_ref=codes.at[u],
            dst_ref=v_ref.at[tm, at],
            send_sem=code_send.at[u],
            recv_sem=code_recv.at[tm, at],
            device_id=device(y, x, zh, to),
            device_id_type=MESH,
        )

    def code_here(u, at):
        return pltpu.make_async_copy(codes.at[u], v_ref.at[tm, at], code_local.at[at])

    mine.start(own_share)
    mine.first()
    across.wait_recv()
    other.start()
    mine.forward(0)
    mine.second()
    other.first()
    mine.forward(1)
    other.forward(0)
    other.second()
    other.forward(1)
    own_m.wait()
    for c in exchanged:
        c.wait_recv()

    def channel(j, carry):
        rows = pl.ds(pl.multiple_of(j * KB, KB), KB)
        for p, part in enumerate((ra, rq)):
            part[rows, :] = y_out[j, p].astype(f32).T
        return carry

    lax.fori_loop(0, CH, channel, 0)
    mine.forward(2)
    other.forward(2)
    own.wait()
    landed(0)
    landed(1)

    def last():
        mine.forward(3)
        other.forward(3)

    group(0, last)
    landed(2)
    landed(3)
    group(1, lambda: None)

    scale_out = [
        remote(
            scales.at[t],
            d_ref.at[tm],
            send.at[97 + d],
            recv.at[97 + d],
            device(y, x, zh, t),
        )
        for d, t in enumerate(tms)
    ]
    own_d = pltpu.make_async_copy(scales.at[tm], d_ref.at[tm], local.at[11])
    own_d.start()

    def flags_of(block):
        rows = pl.ds(SRC * KB, CH // 2)
        return jnp.concatenate(
            [o_ref[lax.rem(block, 2), block // 2, rows, pl.ds(i * 128, 128)] for i in range(2)]
        )

    fr = flags_of(lax.axis_index("chan"))
    fr = jnp.concatenate([fr] * 4, axis=0)
    for b in range(SRC):
        count = lax.dot_general(
            flags_of(plan[b]), fr, (((1,), (1,)), ((), ())), preferred_element_type=f32
        )
        inv[pl.ds(b * CH, CH), :] = 1.0 / jnp.maximum(count, 1.0)
    inv_ref[...] = jnp.zeros_like(inv_ref)
    for i in range(12):
        inv_ref[pl.ds(i, 1), :] = inv[pl.ds(tm * 12 + i, 1), :]

    for t in tms:
        for i in range(3):
            pltpu.make_async_remote_copy(
                src_ref=codes.at[i],
                dst_ref=v_ref.at[t, i],
                send_sem=code_send.at[i],
                recv_sem=code_recv.at[t, i],
                device_id=device(y, x, zh, t),
                device_id_type=MESH,
            ).wait_recv()
            code_to(t * 3 + i, t, i).wait_send()
    for i in range(3):
        code_here(tm * 3 + i, i).wait()
    for c in scale_out:
        c.wait()
    own_d.wait()
    for c in tables:
        c.wait()
    for c in stage_1 + stage_2 + [across] + flags + shares + exchanged + started:
        c.wait_send()


def stack(plan, m, seeds):
    bf, f32 = jnp.bfloat16, jnp.float32
    hbm, vmem = pl.BlockSpec(memory_space=ANY), pl.BlockSpec(memory_space=pltpu.VMEM)
    table = (2, 2, BINS // 32, 16, BINS)
    return pl.pallas_call(
        stack_body,
        out_shape=(
            jax.ShapeDtypeStruct((NTM, 3, 4, 2 * CH, KB), jnp.int16),
            jax.ShapeDtypeStruct((NTM, 16, KB), f32),
            jax.ShapeDtypeStruct((16, 128), f32),
            jax.ShapeDtypeStruct(table, bf),
            jax.ShapeDtypeStruct(table, bf),
        ),
        in_specs=[pl.BlockSpec(memory_space=pltpu.SMEM), hbm, vmem, vmem, vmem, vmem],
        out_specs=(hbm, hbm, vmem, hbm, hbm),
        scratch_shapes=[
            pltpu.VMEM((2, 4, 4, 2, SEG, BINS), bf),
            pltpu.VMEM((2, SRC, 4, 2, SEG, BINS), bf),
            pltpu.VMEM((2, 4, SRC, 2, SEG, BINS), bf),
            pltpu.VMEM((2, SRC, 2, SEG, BINS), bf),
            pltpu.VMEM((NTM * SEG, KB), bf),
            pltpu.VMEM((2, SRC, 2, NTM * SEG, KB), bf),
            pltpu.VMEM((ROWS, 256), bf),
            pltpu.VMEM((CH, 2, NTM * SEG, KB), bf),
            pltpu.VMEM((2, 16, ROWS, 256), bf),
            pltpu.VMEM((HALF * KB, 128), f32),
            pltpu.VMEM((HALF * KB, 128), f32),
            pltpu.VMEM((CH * KB, 128), f32),
            pltpu.VMEM((CH * KB, 128), f32),
            pltpu.VMEM((HALF * KB, 128), f32),
            pltpu.VMEM((SRC * CH, 128), f32),
            pltpu.VMEM((24, 4, 2 * CH, KB), jnp.int16),
            pltpu.VMEM((NTM, 16, KB), f32),
            pltpu.VMEM(table, bf),
            pltpu.VMEM(table, bf),
            pltpu.SemaphoreType.DMA((104,)),
            pltpu.SemaphoreType.DMA((104,)),
            pltpu.SemaphoreType.DMA((12,)),
            pltpu.SemaphoreType.DMA((24,)),
            pltpu.SemaphoreType.DMA((NTM, 3)),
            pltpu.SemaphoreType.DMA((3,)),
        ],
        compiler_params=pltpu.CompilerParams(
            collective_id=0, has_side_effects=True, vmem_limit_bytes=BIG
        ),
    )(plan, m, *seeds)


def make_seeds():
    tau = np.arange(BINS)

    def pair(freq):
        angle = (np.multiply.outer(freq, tau) % (2 * BINS)) * (math.pi / BINS)
        return np.cos(angle), np.sin(angle)

    c1, s1 = pair(np.arange(BINS // 32) * 32)
    c2, s2 = pair(np.add.outer(np.arange(2), 2 * np.arange(16)))
    scale = 1.0 / math.sqrt(BINS)
    return [jnp.asarray(v, jnp.float32) for v in (c1, s1, c2 * scale, s2 * scale)]


def lags_body(v_ref, c_ref, inv_ref, th_ref, tl_ref, out_ref, xh, xl, factor):
    step = th_ref.shape[2]

    @pl.when(pl.program_id(0) == 0)
    def _():
        lane = lax.broadcasted_iota(jnp.int32, (CH, KB), 1)
        for j in range(NTM):
            factor[j] = (c_ref[j] * inv_ref[...]).T

        for s in range(12):
            rows = pl.ds(s * CH, CH)
            for p in range(2):
                for j in range(NTM // 2):
                    a, b = (
                        v_ref[2 * j + i, s, p].astype(jnp.int32).astype(jnp.float32)
                        * factor[2 * j + i, pl.ds(p * CH, CH), s : s + 1]
                        for i in range(2)
                    )
                    even = jnp.where(lane < KB // 2, a, pltpu.roll(b, KB // 2, 1))
                    odd = jnp.where(lane < KB // 2, pltpu.roll(a, KB // 2, 1), b)
                    lanes = pl.ds(p * (BINS // 2) + j * KB, KB)
                    for parity, value in enumerate((even, odd)):
                        high = value.astype(jnp.bfloat16)
                        xh[parity, rows, lanes] = high
                        xl[parity, rows, lanes] = (value - high.astype(jnp.float32)).astype(
                            jnp.bfloat16
                        )

    def dot(a, b):
        return jnp.dot(a, b, preferred_element_type=jnp.float32)

    even, odd = (
        dot(xl[i], th_ref[i]) + dot(xh[i], tl_ref[i]) + dot(xh[i], th_ref[i]) for i in range(2)
    )
    at = pl.program_id(0) * step
    out_ref[:, pl.ds(pl.multiple_of(at, step), step)] = even - odd
    out_ref[:, pl.ds(pl.multiple_of(at + BINS, step), step)] = even + odd


def lags(v, c, inv, th, tl):
    rows, step = 12 * CH, 256
    return pl.pallas_call(
        lags_body,
        grid=(BINS // step,),
        out_shape=jax.ShapeDtypeStruct((rows, 2 * BINS), jnp.float32),
        in_specs=[
            pl.BlockSpec((NTM, 12, 2, CH, KB), lambda g: (0, 0, 0, 0, 0)),
            pl.BlockSpec((NTM, 16, KB), lambda g: (0, 0, 0)),
            pl.BlockSpec((16, 128), lambda g: (0, 0)),
            pl.BlockSpec((2, BINS, step), lambda g: (0, 0, g)),
            pl.BlockSpec((2, BINS, step), lambda g: (0, 0, g)),
        ],
        out_specs=pl.BlockSpec((rows, 2 * BINS), lambda g: (0, 0)),
        scratch_shapes=[
            pltpu.VMEM((2, rows, BINS), jnp.bfloat16),
            pltpu.VMEM((2, rows, BINS), jnp.bfloat16),
            pltpu.VMEM((NTM, 128, 16), jnp.float32),
        ],
        compiler_params=pltpu.CompilerParams(vmem_limit_bytes=BIG),
    )(v, c, inv, th, tl)


def shards(spectra, quality, plan):
    flags = quality.astype(jnp.bfloat16)
    masked = (spectra * flags[:, :, None, None]).transpose(0, 2, 1, 3)
    row = jnp.tile(jnp.pad(flags.T, ((0, 0), (0, KB - CH))), (1, NTM))
    m = jnp.concatenate([masked, jnp.broadcast_to(row, (1, 2, SEG, BINS))], axis=0)
    v, c, inv, th, tl = stack(plan, m, make_seeds())
    th, tl = (t.reshape(2, BINS, BINS) for t in (th, tl))
    out = lags(v.reshape(NTM, 12, 2, CH, KB), c, inv, th, tl)
    return out.reshape(12, CH, 2 * BINS)


def solution(mesh):
    in_specs = (P("chan", "tm", None, None), P("chan", "tm"), P())
    out_specs = P("tm", "chan", None)
    return jax.shard_map(shards, mesh=mesh, in_specs=in_specs, out_specs=out_specs, check_vma=False)
```

```python
import functools
import math

import jax
import jax.numpy as jnp
from jax import lax
from jax.experimental import pallas as pl
from jax.experimental.pallas import tpu as pltpu
from jax.sharding import PartitionSpec as P
import numpy as np

MESH = pl.DeviceIdType.MESH
ANY = pl.ANY
SRC = 3
NX = NY = 4
NTM = 8
CH = 32
SEG = 16
BINS = 1024
KB = BINS // NTM
ROWS = SRC * KB + CH // 2
HALF = 48
EARLY = 16
TOP = 32766.0
BIG = 56 * 1024 * 1024


def place():
    ch = lax.axis_index("chan")
    return ch // 8, lax.rem(ch // 2, 4), lax.rem(ch, 2), lax.axis_index("tm")


def device(y, x, zh, tm):
    return ((y * 4 + x) * 2 + zh, tm)


def up(v, d):
    return lax.rem(v + d, 4)


def greet(devices):
    bar = pltpu.get_barrier_semaphore()
    for d in devices:
        pl.semaphore_signal(bar, inc=1, device_id=d, device_id_type=MESH)
    pl.semaphore_wait(bar, len(devices))


def remote(src, dst, send, recv, where):
    copy = pltpu.make_async_remote_copy(
        src_ref=src, dst_ref=dst, send_sem=send, recv_sem=recv, device_id=where, device_id_type=MESH
    )
    copy.start()
    return copy


def stack_body(
    plan, m, fl, c1, n1, c2, n2, v_ref, d_ref, inv_ref, th_ref, tl_ref,
    r1, s1, r2, s2, fb, yb, own_share, y_out, o_ref, sa, sq, ra, rq, ob, inv, codes, scales, th, tl,
    send, recv, local, code_send, code_recv, code_local,
):
    f32, bf = jnp.float32, jnp.bfloat16
    y, x, zh, tm = place()
    tms = [lax.rem(tm + d, NTM) for d in range(1, NTM)]
    greet(
        [device(y, x, zh, t) for t in tms]
        + [device(y, up(x, d), zh, tm) for d in (1, 2, 3)]
        + [device(up(y, d), x, zh, tm) for d in (1, 2, 3)]
        + [device(y, x, 1 - zh, t) for t in tms + [tm]]
    )
    ox = [lax.rem(plan[b] // 2, 4) for b in range(SRC)]
    oy = [plan[b] // 8 for b in range(SRC)]
    oz = [lax.rem(plan[b], 2) for b in range(SRC)]
    my_lanes = pl.ds(pl.multiple_of(tm * KB, KB), KB)
    my_rows = pl.ds(pl.multiple_of(tm * SEG, SEG), SEG)

    def bins_of(t):
        return pl.ds(pl.multiple_of(t * KB, KB), KB)

    def main(first, count, base):
        return [
            remote(
                m.at[pl.ds(first, count), :, :, bins_of(tms[d - 1])],
                y_out.at[pl.ds(first, count), :, my_rows, :],
                send.at[base + d],
                recv.at[base + d],
                device(y, x, zh, tms[d - 1]),
            )
            for d in range(1, NTM)
        ]

    def first_to(h, d):
        return (y, up(x, d)) if h == 0 else (up(y, d), x)

    def second_to(h, d):
        return first_to(1 - h, d)

    first_at, second_at = (x, y), (y, x)
    first_owner, second_owner = (ox, oy), (oy, ox)
    stage_1 = []
    for d in (1, 3, 2):
        for h in range(2):
            to = first_to(h, d)
            piece = pl.ds(16 * h + 4 * up(first_at[h], d), 4)
            stage_1.append(
                remote(
                    m.at[piece],
                    r1.at[h, first_at[h]],
                    send.at[3 * h + d],
                    recv.at[3 * h + d],
                    device(*to, zh, tm),
                )
            )
    own_1 = [
        pltpu.make_async_copy(
            m.at[pl.ds(16 * h + 4 * first_at[h], 4)], r1.at[h, first_at[h]], local.at[7 + h]
        )
        for h in range(2)
    ]
    for c in own_1:
        c.start()
    flags = [
        remote(
            fl,
            fb.at[my_rows, :],
            send.at[24 + d],
            recv.at[24 + d],
            device(y, x, zh, t),
        )
        for d, t in enumerate(tms, 1)
    ]
    own_f = pltpu.make_async_copy(fl, fb.at[my_rows, :], local.at[5])
    own_f.start()
    exchanged = main(0, EARLY, 73)
    own_m = pltpu.make_async_copy(
        m.at[:, :, :, my_lanes], y_out.at[:, :, my_rows, :], local.at[1]
    )
    own_m.start()

    def make(e1, carry):
        cos1 = jnp.broadcast_to(c1[pl.ds(e1, 1), :], (16, BINS))
        sin1 = jnp.broadcast_to(n1[pl.ds(e1, 1), :], (16, BINS))
        for parity in range(2):
            cos = cos1 * c2[parity] - sin1 * n2[parity]
            sin = -(sin1 * c2[parity] + cos1 * n2[parity])
            for p, value in enumerate((cos, sin)):
                high = value.astype(bf)
                th[parity, p, e1] = high
                tl[parity, p, e1] = (value - high.astype(f32)).astype(bf)
        return carry

    lax.fori_loop(0, BINS // 32, make, 0)
    tables = [
        pltpu.make_async_copy(th, th_ref, local.at[9]),
        pltpu.make_async_copy(tl, tl_ref, local.at[10]),
    ]
    for c in tables:
        c.start()
    scales[...] = jnp.zeros_like(scales)

    for c in own_1:
        c.wait()
    for c in stage_1:
        c.wait_recv()
    for h in range(2):
        for b in range(SRC):

            def pick(i, carry, h=h, b=b):
                s1[h, b, i] = r1[h, first_owner[h][b], i]
                return carry

            lax.fori_loop(0, 4, pick, 0)
    stage_2 = []
    for d in (1, 3, 2):
        for h in range(2):
            to = second_to(h, d)
            stage_2.append(
                remote(
                    s1.at[h, :, up(second_at[h], d)],
                    r2.at[h, second_at[h]],
                    send.at[6 + 3 * h + d],
                    recv.at[6 + 3 * h + d],
                    device(*to, zh, tm),
                )
            )
    own_2 = [
        pltpu.make_async_copy(
            s1.at[h, :, second_at[h]], r2.at[h, second_at[h]], local.at[2 * h]
        )
        for h in range(2)
    ]
    for c in own_2:
        c.start()
    for c in own_2:
        c.wait()
    for c in stage_2:
        c.wait_recv()
    for h in range(2):
        for b in range(SRC):
            s2[h, b] = r2[h, second_owner[h][b], b]
    shares = []
    for other in range(2):
        half = zh + other * (1 - 2 * zh)
        for d in range(1 - other, NTM):
            t = lax.rem(tm + d, NTM)
            k = 81 + 8 * other + d
            shares.append(
                remote(
                    s2.at[half, :, :, :, bins_of(t)],
                    yb.at[zh, :, :, my_rows, :],
                    send.at[k],
                    recv.at[k],
                    device(y, x, half, t),
                )
            )
    own_s = pltpu.make_async_copy(
        s2.at[zh, :, :, :, my_lanes], yb.at[zh, :, :, my_rows, :], local.at[4]
    )
    own_s.start()
    own_s.wait()
    own_f.wait()
    for c in flags + shares:
        c.wait_recv()

    for p in range(2):
        lanes = pl.ds(p * 128, 128)
        for b in range(SRC):
            part = yb[oz[b], b, p].astype(jnp.float32).T
            own_share[pl.ds(b * KB, KB), lanes] = part.astype(jnp.bfloat16)
    part = fb[...].astype(jnp.float32).T.astype(jnp.bfloat16)
    for i in range(2):
        own_share[pl.ds(SRC * KB, CH // 2), pl.ds(i * 128, 128)] = part[i * 16 : i * 16 + 16]

    cut = ROWS // 32 * 16
    me = y * 4 + x
    across = remote(
        own_share, o_ref.at[zh, me], send.at[32], recv.at[32], device(y, x, 1 - zh, tm)
    )
    own = pltpu.make_async_copy(own_share, o_ref.at[zh, me], local.at[6])
    own.start()
    started = []
    full, low, high = pl.ds(0, ROWS), pl.ds(0, cut), pl.ds(cut, ROWS - cut)

    class Half:
        def __init__(self, half):
            self.half = half
            ay, ax = half, 1 - half
            self.ap = device(up(y, ay), up(x, ax), zh, tm)
            self.am = device(up(y, 3 * ay), up(x, 3 * ax), zh, tm)
            self.bp = device(up(y, ax), up(x, ay), zh, tm)
            self.bm = device(up(y, 3 * ax), up(x, 3 * ay), zh, tm)
            self.a = x * ax + y * ay
            self.b = x * ay + y * ax
            self.base = 33 + 20 * half
            self.sent = {}
            self.passed = {}

        def put(self, b, a, part, k, where, source=None):
            slot = b * (4 - 3 * self.half) + a * (1 + 3 * self.half)
            ref = o_ref.at[self.half, slot, part]
            k = self.base + k
            copy = remote(ref if source is None else source, ref, send.at[k], recv.at[k], where)
            started.append(copy)
            return copy

        def at(self, r):
            return up(self.a, (0, 3, 1, 2)[r])

        def send_b(self, r, source=None):
            k = 4 + 4 * r
            self.sent[r] = (
                self.put(self.b, self.at(r), full, k, self.bp, source),
                self.put(self.b, self.at(r), full, k + 1, self.bm, source),
            )

        def start(self, source=None):
            self.a1 = self.put(self.b, self.a, full, 0, self.ap, source)
            self.a2 = self.put(self.b, self.a, full, 1, self.am, source)
            self.send_b(0, source)

        def first(self):
            self.a1.wait_recv()
            self.a3 = self.put(self.b, self.at(1), low, 2, self.ap)
            self.send_b(1)
            self.a2.wait_recv()
            self.a4 = self.put(self.b, self.at(2), high, 3, self.am)
            self.send_b(2)

        def second(self):
            self.a3.wait_recv()
            self.a4.wait_recv()
            self.send_b(3)

        def forward(self, r):
            k = 4 + 4 * r
            plus, minus = self.sent[r]
            plus.wait_recv()
            f1 = self.put(up(self.b, 3), self.at(r), low, k + 2, self.bp)
            minus.wait_recv()
            f2 = self.put(up(self.b, 1), self.at(r), high, k + 3, self.bm)
            self.passed[r] = (f1, f2)

    mine, other = Half(zh), Half(1 - zh)

    def landed(r):
        for h in (mine, other):
            for f in h.passed[r]:
                f.wait_recv()

    def group(count, first, step, between, during):
        size = 24 * count

        def coords(q):
            blk, h, ri = q // (2 * count), lax.rem(q // count, 2), lax.rem(q, count)
            return blk, h, up(x + h * (y - x), first + step * ri)

        def widen(q, carry):
            blk, h, a = coords(q)
            for bb in range(4):
                rows = pl.ds(pl.multiple_of((q * 4 + bb) * KB, KB), KB)
                slot = bb * (4 - 3 * h) + a * (1 + 3 * h)
                tile = pl.ds(pl.multiple_of(blk * KB, KB), KB)
                for p, part in enumerate((sa, sq)):
                    part[rows, :] = o_ref[h, slot, tile, pl.ds(p * 128, 128)].astype(f32)
            return carry

        lax.fori_loop(0, 6 * count, widen, 0)
        between()

        def one(k, to):
            sources, channels = pl.ds(k, size, stride=KB), pl.ds(k, CH, stride=KB)
            s = jnp.concatenate([sa[sources, :], sq[sources, :]], axis=1).astype(bf)
            a, q = ra[channels, :], rq[channels, :]
            real, imag = jnp.concatenate([a, q], axis=1), jnp.concatenate([q, -a], axis=1)
            both = jnp.concatenate([real, imag], axis=0).astype(bf)
            res = lax.dot_general(s, both, (((1,), (1,)), ((), ())), preferred_element_type=f32)
            ob[pl.ds(to, size, stride=KB), :] = jnp.concatenate([res, jnp.zeros_like(res)], axis=1)

        def some(i, carry):
            for t in range(8):
                one(i * 8 + t, i * 4 + t // 2 + t % 2 * (KB // 2))
            return carry

        lax.fori_loop(0, KB // 16, some, 0)
        during()
        lax.fori_loop(KB // 16, KB // 8, some, 0)

        def turn(q, carry):
            blk, h, a = coords(q)
            u = 8 * blk + 4 * h + a
            to, at = u // 3, lax.rem(u, 3)
            for bb in range(4):
                block = ob[pl.ds(pl.multiple_of((q * 4 + bb) * KB, KB), KB), :]
                most = jnp.maximum(jnp.max(jnp.abs(block), axis=0, keepdims=True), 1e-30)
                code = jnp.round(block * (TOP / most)).T[: 2 * CH]
                codes[u, bb] = code.astype(jnp.int32).astype(jnp.int16)
                scales[to, pl.ds(at * 4 + bb, 1), :] = most * (1.0 / TOP)

            @pl.when(to != tm)
            def _():
                code_to(u, to, at).start()

            @pl.when(to == tm)
            def _():
                code_here(u, at).start()

            return carry

        lax.fori_loop(0, 6 * count, turn, 0)

    def code_to(u, to, at):
        return pltpu.make_async_remote_copy(
            src_ref=codes.at[u],
            dst_ref=v_ref.at[tm, at],
            send_sem=code_send.at[u],
            recv_sem=code_recv.at[tm, at],
            device_id=device(y, x, zh, to),
            device_id_type=MESH,
        )

    def code_here(u, at):
        return pltpu.make_async_copy(codes.at[u], v_ref.at[tm, at], code_local.at[at])

    mine.start(own_share)
    exchanged += main(EARLY, CH - EARLY, 15)
    mine.first()
    across.wait_recv()
    other.start()
    mine.forward(0)
    mine.second()
    other.first()
    mine.forward(1)
    other.forward(0)
    other.second()
    other.forward(1)
    own_m.wait()
    for c in exchanged:
        c.wait_recv()

    def channel(j, carry):
        rows = pl.ds(pl.multiple_of(j * KB, KB), KB)
        for p, part in enumerate((ra, rq)):
            part[rows, :] = y_out[j, p].astype(f32).T
        return carry

    lax.fori_loop(0, CH, channel, 0)
    mine.forward(2)
    own.wait()
    landed(0)
    group(1, 0, 0, lambda: other.forward(2), lambda: mine.forward(3))
    landed(1)
    landed(2)
    group(2, 3, -2, lambda: other.forward(3), lambda: None)
    landed(3)
    group(1, 2, 0, lambda: None, lambda: None)

    scale_out = [
        remote(
            scales.at[t],
            d_ref.at[tm],
            send.at[97 + d],
            recv.at[97 + d],
            device(y, x, zh, t),
        )
        for d, t in enumerate(tms)
    ]
    own_d = pltpu.make_async_copy(scales.at[tm], d_ref.at[tm], local.at[11])
    own_d.start()

    def flags_of(block):
        rows = pl.ds(SRC * KB, CH // 2)
        return jnp.concatenate(
            [o_ref[lax.rem(block, 2), block // 2, rows, pl.ds(i * 128, 128)] for i in range(2)]
        )

    fr = flags_of(lax.axis_index("chan"))
    fr = jnp.concatenate([fr] * 4, axis=0)
    for b in range(SRC):
        count = lax.dot_general(
            flags_of(plan[b]), fr, (((1,), (1,)), ((), ())), preferred_element_type=f32
        )
        inv[pl.ds(b * CH, CH), :] = 1.0 / jnp.maximum(count, 1.0)
    inv_ref[...] = jnp.zeros_like(inv_ref)
    for i in range(12):
        inv_ref[pl.ds(i, 1), :] = inv[pl.ds(tm * 12 + i, 1), :]

    for t in tms:
        for i in range(3):
            pltpu.make_async_remote_copy(
                src_ref=codes.at[i],
                dst_ref=v_ref.at[t, i],
                send_sem=code_send.at[i],
                recv_sem=code_recv.at[t, i],
                device_id=device(y, x, zh, t),
                device_id_type=MESH,
            ).wait_recv()
            code_to(t * 3 + i, t, i).wait_send()
    for i in range(3):
        code_here(tm * 3 + i, i).wait()
    for c in scale_out:
        c.wait()
    own_d.wait()
    for c in tables:
        c.wait()
    for c in stage_1 + stage_2 + [across] + flags + shares + exchanged + started:
        c.wait_send()


def stack(plan, m, fl, seeds):
    bf, f32 = jnp.bfloat16, jnp.float32
    hbm, vmem = pl.BlockSpec(memory_space=ANY), pl.BlockSpec(memory_space=pltpu.VMEM)
    table = (2, 2, BINS // 32, 16, BINS)
    return pl.pallas_call(
        stack_body,
        out_shape=(
            jax.ShapeDtypeStruct((NTM, 3, 4, 2 * CH, KB), jnp.int16),
            jax.ShapeDtypeStruct((NTM, 16, KB), f32),
            jax.ShapeDtypeStruct((16, 128), f32),
            jax.ShapeDtypeStruct(table, bf),
            jax.ShapeDtypeStruct(table, bf),
        ),
        in_specs=[pl.BlockSpec(memory_space=pltpu.SMEM), hbm, vmem, vmem, vmem, vmem, vmem],
        out_specs=(hbm, hbm, vmem, hbm, hbm),
        scratch_shapes=[
            pltpu.VMEM((2, 4, 4, 2, SEG, BINS), bf),
            pltpu.VMEM((2, SRC, 4, 2, SEG, BINS), bf),
            pltpu.VMEM((2, 4, SRC, 2, SEG, BINS), bf),
            pltpu.VMEM((2, SRC, 2, SEG, BINS), bf),
            pltpu.VMEM((NTM * SEG, KB), bf),
            pltpu.VMEM((2, SRC, 2, NTM * SEG, KB), bf),
            pltpu.VMEM((ROWS, 256), bf),
            pltpu.VMEM((CH, 2, NTM * SEG, KB), bf),
            pltpu.VMEM((2, 16, ROWS, 256), bf),
            pltpu.VMEM((HALF * KB, 128), f32),
            pltpu.VMEM((HALF * KB, 128), f32),
            pltpu.VMEM((CH * KB, 128), f32),
            pltpu.VMEM((CH * KB, 128), f32),
            pltpu.VMEM((HALF * KB, 128), f32),
            pltpu.VMEM((SRC * CH, 128), f32),
            pltpu.VMEM((24, 4, 2 * CH, KB), jnp.int16),
            pltpu.VMEM((NTM, 16, KB), f32),
            pltpu.VMEM(table, bf),
            pltpu.VMEM(table, bf),
            pltpu.SemaphoreType.DMA((104,)),
            pltpu.SemaphoreType.DMA((104,)),
            pltpu.SemaphoreType.DMA((12,)),
            pltpu.SemaphoreType.DMA((24,)),
            pltpu.SemaphoreType.DMA((NTM, 3)),
            pltpu.SemaphoreType.DMA((3,)),
        ],
        compiler_params=pltpu.CompilerParams(
            collective_id=0, has_side_effects=True, vmem_limit_bytes=BIG
        ),
    )(plan, m, fl, *seeds)


def make_seeds():
    tau = np.arange(BINS)

    def pair(freq):
        angle = (np.multiply.outer(freq, tau) % (2 * BINS)) * (math.pi / BINS)
        return np.cos(angle), np.sin(angle)

    c1, s1 = pair(np.arange(BINS // 32) * 32)
    c2, s2 = pair(np.add.outer(np.arange(2), 2 * np.arange(16)))
    scale = 1.0 / math.sqrt(BINS)
    return [jnp.asarray(v, jnp.float32) for v in (c1, s1, c2 * scale, s2 * scale)]


def lags_body(v_ref, c_ref, inv_ref, th_ref, tl_ref, out_ref, xh, xl, factor):
    step = th_ref.shape[2]

    @pl.when(pl.program_id(0) == 0)
    def _():
        lane = lax.broadcasted_iota(jnp.int32, (CH, KB), 1)
        for j in range(NTM):
            factor[j] = (c_ref[j] * inv_ref[...]).T

        def split(q, carry):
            p, j = q // 4, lax.rem(q, 4)
            lanes = pl.ds(pl.multiple_of(q * KB, KB), KB)
            part = pl.ds(pl.multiple_of(p * CH, CH), CH)
            for s in range(12):
                rows = pl.ds(s * CH, CH)
                a, b = (
                    v_ref[2 * j + i, s, p].astype(jnp.int32).astype(jnp.float32)
                    * factor[2 * j + i, part, s : s + 1]
                    for i in range(2)
                )
                even = jnp.where(lane < KB // 2, a, pltpu.roll(b, KB // 2, 1))
                odd = jnp.where(lane < KB // 2, pltpu.roll(a, KB // 2, 1), b)
                for parity, value in enumerate((even, odd)):
                    high = value.astype(jnp.bfloat16)
                    xh[parity, rows, lanes] = high
                    xl[parity, rows, lanes] = (value - high.astype(jnp.float32)).astype(
                        jnp.bfloat16
                    )
            return carry

        lax.fori_loop(0, 2 * NTM // 2, split, 0)

    def dot(a, b):
        return jnp.dot(a, b, preferred_element_type=jnp.float32)

    even, odd = (
        dot(xl[i], th_ref[i]) + dot(xh[i], tl_ref[i]) + dot(xh[i], th_ref[i]) for i in range(2)
    )
    at = pl.program_id(0) * step
    out_ref[:, pl.ds(pl.multiple_of(at, step), step)] = even - odd
    out_ref[:, pl.ds(pl.multiple_of(at + BINS, step), step)] = even + odd


def lags(v, c, inv, th, tl):
    rows, step = 12 * CH, 256
    return pl.pallas_call(
        lags_body,
        grid=(BINS // step,),
        out_shape=jax.ShapeDtypeStruct((rows, 2 * BINS), jnp.float32),
        in_specs=[
            pl.BlockSpec((NTM, 12, 2, CH, KB), lambda g: (0, 0, 0, 0, 0)),
            pl.BlockSpec((NTM, 16, KB), lambda g: (0, 0, 0)),
            pl.BlockSpec((16, 128), lambda g: (0, 0)),
            pl.BlockSpec((2, BINS, step), lambda g: (0, 0, g)),
            pl.BlockSpec((2, BINS, step), lambda g: (0, 0, g)),
        ],
        out_specs=pl.BlockSpec((rows, 2 * BINS), lambda g: (0, 0)),
        scratch_shapes=[
            pltpu.VMEM((2, rows, BINS), jnp.bfloat16),
            pltpu.VMEM((2, rows, BINS), jnp.bfloat16),
            pltpu.VMEM((NTM, 128, 16), jnp.float32),
        ],
        compiler_params=pltpu.CompilerParams(vmem_limit_bytes=BIG),
    )(v, c, inv, th, tl)


def shards(spectra, quality, plan):
    flags = quality.astype(jnp.bfloat16)
    m = (spectra * flags[:, :, None, None]).transpose(0, 2, 1, 3)
    fl = jnp.pad(flags.T, ((0, 0), (0, KB - CH)))
    v, c, inv, th, tl = stack(plan, m, fl, make_seeds())
    th, tl = (t.reshape(2, BINS, BINS) for t in (th, tl))
    out = lags(v.reshape(NTM, 12, 2, CH, KB), c, inv, th, tl)
    return out.reshape(12, CH, 2 * BINS)


def solution(mesh):
    in_specs = (P("chan", "tm", None, None), P("chan", "tm"), P())
    out_specs = P("tm", "chan", None)
    return jax.shard_map(shards, mesh=mesh, in_specs=in_specs, out_specs=out_specs, check_vma=False)
```

```python
import functools
import math

import jax
import jax.numpy as jnp
from jax import lax
from jax.experimental import pallas as pl
from jax.experimental.pallas import tpu as pltpu
from jax.sharding import PartitionSpec as P
import numpy as np

MESH = pl.DeviceIdType.MESH
ANY = pl.ANY
SRC = 3
NX = NY = 4
NTM = 8
CH = 32
SEG = 16
BINS = 1024
KB = BINS // NTM
ROWS = SRC * KB + CH // 2
HALF = 48
EARLY = 16
TOP = 32766.0
BIG = 56 * 1024 * 1024


def place():
    ch = lax.axis_index("chan")
    return ch // 8, lax.rem(ch // 2, 4), lax.rem(ch, 2), lax.axis_index("tm")


def device(y, x, zh, tm):
    return ((y * 4 + x) * 2 + zh, tm)


def up(v, d):
    return lax.rem(v + d, 4)


def greet(devices):
    bar = pltpu.get_barrier_semaphore()
    for d in devices:
        pl.semaphore_signal(bar, inc=1, device_id=d, device_id_type=MESH)
    pl.semaphore_wait(bar, len(devices))


def remote(src, dst, send, recv, where):
    copy = pltpu.make_async_remote_copy(
        src_ref=src, dst_ref=dst, send_sem=send, recv_sem=recv, device_id=where, device_id_type=MESH
    )
    copy.start()
    return copy


def stack_body(
    plan, m, fl, c1, n1, c2, n2, v_ref, d_ref, inv_ref, th_ref, tl_ref,
    r1, s1, r2, s2, fb, yb, own_share, y_out, o_ref, sa, sq, ra, rq, turned, ob, inv, codes, scales, th, tl,
    send, recv, local, code_send, code_recv, code_local,
):
    f32, bf = jnp.float32, jnp.bfloat16
    y, x, zh, tm = place()
    tms = [lax.rem(tm + d, NTM) for d in range(1, NTM)]
    greet(
        [device(y, x, zh, t) for t in tms]
        + [device(y, up(x, d), zh, tm) for d in (1, 2, 3)]
        + [device(up(y, d), x, zh, tm) for d in (1, 2, 3)]
        + [device(y, x, 1 - zh, t) for t in tms + [tm]]
    )
    ox = [lax.rem(plan[b] // 2, 4) for b in range(SRC)]
    oy = [plan[b] // 8 for b in range(SRC)]
    oz = [lax.rem(plan[b], 2) for b in range(SRC)]
    my_lanes = pl.ds(pl.multiple_of(tm * KB, KB), KB)
    my_rows = pl.ds(pl.multiple_of(tm * SEG, SEG), SEG)

    def bins_of(t):
        return pl.ds(pl.multiple_of(t * KB, KB), KB)

    def main(first, count, base):
        return [
            remote(
                m.at[pl.ds(first, count), :, :, bins_of(tms[d - 1])],
                y_out.at[pl.ds(first, count), :, my_rows, :],
                send.at[base + d],
                recv.at[base + d],
                device(y, x, zh, tms[d - 1]),
            )
            for d in range(1, NTM)
        ]

    def first_to(h, d):
        return (y, up(x, d)) if h == 0 else (up(y, d), x)

    def second_to(h, d):
        return first_to(1 - h, d)

    first_at, second_at = (x, y), (y, x)
    first_owner, second_owner = (ox, oy), (oy, ox)
    stage_1 = []
    for d in (1, 3, 2):
        for h in range(2):
            to = first_to(h, d)
            piece = pl.ds(16 * h + 4 * up(first_at[h], d), 4)
            stage_1.append(
                remote(
                    m.at[piece],
                    r1.at[h, first_at[h]],
                    send.at[3 * h + d],
                    recv.at[3 * h + d],
                    device(*to, zh, tm),
                )
            )
    own_1 = [
        pltpu.make_async_copy(
            m.at[pl.ds(16 * h + 4 * first_at[h], 4)], r1.at[h, first_at[h]], local.at[7 + h]
        )
        for h in range(2)
    ]
    for c in own_1:
        c.start()
    flags = [
        remote(
            fl,
            fb.at[my_rows, :],
            send.at[24 + d],
            recv.at[24 + d],
            device(y, x, zh, t),
        )
        for d, t in enumerate(tms, 1)
    ]
    own_f = pltpu.make_async_copy(fl, fb.at[my_rows, :], local.at[5])
    own_f.start()
    exchanged = main(0, EARLY, 73)
    own_m = pltpu.make_async_copy(
        m.at[:, :, :, my_lanes], y_out.at[:, :, my_rows, :], local.at[1]
    )
    own_m.start()

    def make(e1, carry):
        cos1 = jnp.broadcast_to(c1[pl.ds(e1, 1), :], (16, BINS))
        sin1 = jnp.broadcast_to(n1[pl.ds(e1, 1), :], (16, BINS))
        for parity in range(2):
            cos = cos1 * c2[parity] - sin1 * n2[parity]
            sin = -(sin1 * c2[parity] + cos1 * n2[parity])
            for p, value in enumerate((cos, sin)):
                high = value.astype(bf)
                th[parity, p, e1] = high
                tl[parity, p, e1] = (value - high.astype(f32)).astype(bf)
        return carry

    lax.fori_loop(0, BINS // 32, make, 0)
    tables = [
        pltpu.make_async_copy(th, th_ref, local.at[9]),
        pltpu.make_async_copy(tl, tl_ref, local.at[10]),
    ]
    for c in tables:
        c.start()
    scales[...] = jnp.zeros_like(scales)

    for c in own_1:
        c.wait()
    for c in stage_1:
        c.wait_recv()
    for h in range(2):
        for b in range(SRC):

            def pick(i, carry, h=h, b=b):
                s1[h, b, i] = r1[h, first_owner[h][b], i]
                return carry

            lax.fori_loop(0, 4, pick, 0)
    stage_2 = []
    for d in (1, 3, 2):
        for h in range(2):
            to = second_to(h, d)
            stage_2.append(
                remote(
                    s1.at[h, :, up(second_at[h], d)],
                    r2.at[h, second_at[h]],
                    send.at[6 + 3 * h + d],
                    recv.at[6 + 3 * h + d],
                    device(*to, zh, tm),
                )
            )
    own_2 = [
        pltpu.make_async_copy(
            s1.at[h, :, second_at[h]], r2.at[h, second_at[h]], local.at[2 * h]
        )
        for h in range(2)
    ]
    for c in own_2:
        c.start()
    for c in own_2:
        c.wait()
    for c in stage_2:
        c.wait_recv()
    for h in range(2):
        for b in range(SRC):
            s2[h, b] = r2[h, second_owner[h][b], b]
    shares = []
    for other in range(2):
        half = zh + other * (1 - 2 * zh)
        for d in range(1 - other, NTM):
            t = lax.rem(tm + d, NTM)
            k = 81 + 8 * other + d
            shares.append(
                remote(
                    s2.at[half, :, :, :, bins_of(t)],
                    yb.at[zh, :, :, my_rows, :],
                    send.at[k],
                    recv.at[k],
                    device(y, x, half, t),
                )
            )
    own_s = pltpu.make_async_copy(
        s2.at[zh, :, :, :, my_lanes], yb.at[zh, :, :, my_rows, :], local.at[4]
    )
    own_s.start()
    own_s.wait()
    own_f.wait()
    for c in flags + shares:
        c.wait_recv()

    for p in range(2):
        lanes = pl.ds(p * 128, 128)
        for b in range(SRC):
            part = yb[oz[b], b, p].astype(jnp.float32).T
            own_share[pl.ds(b * KB, KB), lanes] = part.astype(jnp.bfloat16)
    part = fb[...].astype(jnp.float32).T.astype(jnp.bfloat16)
    for i in range(2):
        own_share[pl.ds(SRC * KB, CH // 2), pl.ds(i * 128, 128)] = part[i * 16 : i * 16 + 16]

    cut = ROWS // 32 * 16
    me = y * 4 + x
    across = remote(
        own_share, o_ref.at[zh, me], send.at[32], recv.at[32], device(y, x, 1 - zh, tm)
    )
    own = pltpu.make_async_copy(own_share, o_ref.at[zh, me], local.at[6])
    own.start()
    started = []
    full, low, high = pl.ds(0, ROWS), pl.ds(0, cut), pl.ds(cut, ROWS - cut)

    class Half:
        def __init__(self, half):
            self.half = half
            ay, ax = half, 1 - half
            self.ap = device(up(y, ay), up(x, ax), zh, tm)
            self.am = device(up(y, 3 * ay), up(x, 3 * ax), zh, tm)
            self.bp = device(up(y, ax), up(x, ay), zh, tm)
            self.bm = device(up(y, 3 * ax), up(x, 3 * ay), zh, tm)
            self.a = x * ax + y * ay
            self.b = x * ay + y * ax
            self.base = 33 + 20 * half
            self.sent = {}
            self.passed = {}

        def put(self, b, a, part, k, where, source=None):
            slot = b * (4 - 3 * self.half) + a * (1 + 3 * self.half)
            ref = o_ref.at[self.half, slot, part]
            k = self.base + k
            copy = remote(ref if source is None else source, ref, send.at[k], recv.at[k], where)
            started.append(copy)
            return copy

        def at(self, r):
            return up(self.a, (0, 3, 1, 2)[r])

        def send_b(self, r, source=None):
            k = 4 + 4 * r
            self.sent[r] = (
                self.put(self.b, self.at(r), full, k, self.bp, source),
                self.put(self.b, self.at(r), full, k + 1, self.bm, source),
            )

        def start(self, source=None):
            self.a1 = self.put(self.b, self.a, full, 0, self.ap, source)
            self.a2 = self.put(self.b, self.a, full, 1, self.am, source)
            self.send_b(0, source)

        def first(self):
            self.a1.wait_recv()
            self.a3 = self.put(self.b, self.at(1), low, 2, self.ap)
            self.send_b(1)
            self.a2.wait_recv()
            self.a4 = self.put(self.b, self.at(2), high, 3, self.am)
            self.send_b(2)

        def second(self):
            self.a3.wait_recv()
            self.a4.wait_recv()
            self.send_b(3)

        def forward(self, r):
            k = 4 + 4 * r
            plus, minus = self.sent[r]
            plus.wait_recv()
            f1 = self.put(up(self.b, 3), self.at(r), low, k + 2, self.bp)
            minus.wait_recv()
            f2 = self.put(up(self.b, 1), self.at(r), high, k + 3, self.bm)
            self.passed[r] = (f1, f2)

    mine, other = Half(zh), Half(1 - zh)

    def landed(r):
        for h in (mine, other):
            for f in h.passed[r]:
                f.wait_recv()

    def group(count, first, step, between, during):
        size = 24 * count

        def coords(q):
            blk, h, ri = q // (2 * count), lax.rem(q // count, 2), lax.rem(q, count)
            return blk, h, up(x + h * (y - x), first + step * ri)

        def widen(q, carry):
            blk, h, a = coords(q)
            for bb in range(4):
                rows = pl.ds(pl.multiple_of((q * 4 + bb) * KB, KB), KB)
                slot = bb * (4 - 3 * h) + a * (1 + 3 * h)
                tile = pl.ds(pl.multiple_of(blk * KB, KB), KB)
                for p, part in enumerate((sa, sq)):
                    part[rows, :] = o_ref[h, slot, tile, pl.ds(p * 128, 128)].astype(f32)
            return carry

        lax.fori_loop(0, 6 * count, widen, 0)
        between()

        def one(k, to):
            sources, channels = pl.ds(k, size, stride=KB), pl.ds(k, CH, stride=KB)
            s = jnp.concatenate([sa[sources, :], sq[sources, :]], axis=1).astype(bf)
            if first == 0:
                a, q = ra[channels, :], rq[channels, :]
                real, imag = jnp.concatenate([a, q], axis=1), jnp.concatenate([q, -a], axis=1)
                both = jnp.concatenate([real, imag], axis=0).astype(bf)
                turned[k] = both
            else:
                both = turned[k]
            res = lax.dot_general(s, both, (((1,), (1,)), ((), ())), preferred_element_type=f32)
            ob[pl.ds(to, size, stride=KB), :] = jnp.concatenate([res, jnp.zeros_like(res)], axis=1)

        def some(i, carry):
            for t in range(8):
                one(i * 8 + t, i * 4 + t // 2 + t % 2 * (KB // 2))
            return carry

        lax.fori_loop(0, KB // 16, some, 0)
        during()
        lax.fori_loop(KB // 16, KB // 8, some, 0)

        def turn(q, carry):
            blk, h, a = coords(q)
            u = 8 * blk + 4 * h + a
            to, at = u // 3, lax.rem(u, 3)
            for bb in range(4):
                block = ob[pl.ds(pl.multiple_of((q * 4 + bb) * KB, KB), KB), :]
                most = jnp.maximum(jnp.max(jnp.abs(block), axis=0, keepdims=True), 1e-30)
                code = jnp.round(block * (TOP / most)).T[: 2 * CH]
                codes[u, bb] = code.astype(jnp.int32).astype(jnp.int16)
                scales[to, pl.ds(at * 4 + bb, 1), :] = most * (1.0 / TOP)

            @pl.when(to != tm)
            def _():
                code_to(u, to, at).start()

            @pl.when(to == tm)
            def _():
                code_here(u, at).start()

            return carry

        lax.fori_loop(0, 6 * count, turn, 0)

    def code_to(u, to, at):
        return pltpu.make_async_remote_copy(
            src_ref=codes.at[u],
            dst_ref=v_ref.at[tm, at],
            send_sem=code_send.at[u],
            recv_sem=code_recv.at[tm, at],
            device_id=device(y, x, zh, to),
            device_id_type=MESH,
        )

    def code_here(u, at):
        return pltpu.make_async_copy(codes.at[u], v_ref.at[tm, at], code_local.at[at])

    mine.start(own_share)
    exchanged += main(EARLY, CH - EARLY, 15)
    mine.first()
    across.wait_recv()
    other.start()
    mine.forward(0)
    mine.second()
    other.first()
    mine.forward(1)
    other.forward(0)
    other.second()
    other.forward(1)
    own_m.wait()
    for c in exchanged:
        c.wait_recv()

    def channel(j, carry):
        rows = pl.ds(pl.multiple_of(j * KB, KB), KB)
        for p, part in enumerate((ra, rq)):
            part[rows, :] = y_out[j, p].astype(f32).T
        return carry

    lax.fori_loop(0, CH, channel, 0)
    mine.forward(2)
    own.wait()
    landed(0)
    group(1, 0, 0, lambda: other.forward(2), lambda: mine.forward(3))
    landed(1)
    landed(2)
    group(2, 3, -2, lambda: other.forward(3), lambda: None)
    landed(3)
    group(1, 2, 0, lambda: None, lambda: None)

    scale_out = [
        remote(
            scales.at[t],
            d_ref.at[tm],
            send.at[97 + d],
            recv.at[97 + d],
            device(y, x, zh, t),
        )
        for d, t in enumerate(tms)
    ]
    own_d = pltpu.make_async_copy(scales.at[tm], d_ref.at[tm], local.at[11])
    own_d.start()

    def flags_of(block):
        rows = pl.ds(SRC * KB, CH // 2)
        return jnp.concatenate(
            [o_ref[lax.rem(block, 2), block // 2, rows, pl.ds(i * 128, 128)] for i in range(2)]
        )

    fr = flags_of(lax.axis_index("chan"))
    fr = jnp.concatenate([fr] * 4, axis=0)
    for b in range(SRC):
        count = lax.dot_general(
            flags_of(plan[b]), fr, (((1,), (1,)), ((), ())), preferred_element_type=f32
        )
        inv[pl.ds(b * CH, CH), :] = 1.0 / jnp.maximum(count, 1.0)
    inv_ref[...] = jnp.zeros_like(inv_ref)
    for i in range(12):
        inv_ref[pl.ds(i, 1), :] = inv[pl.ds(tm * 12 + i, 1), :]

    for t in tms:
        for i in range(3):
            pltpu.make_async_remote_copy(
                src_ref=codes.at[i],
                dst_ref=v_ref.at[t, i],
                send_sem=code_send.at[i],
                recv_sem=code_recv.at[t, i],
                device_id=device(y, x, zh, t),
                device_id_type=MESH,
            ).wait_recv()
            code_to(t * 3 + i, t, i).wait_send()
    for i in range(3):
        code_here(tm * 3 + i, i).wait()
    for c in scale_out:
        c.wait()
    own_d.wait()
    for c in tables:
        c.wait()
    for c in stage_1 + stage_2 + [across] + flags + shares + exchanged + started:
        c.wait_send()


def stack(plan, m, fl, seeds):
    bf, f32 = jnp.bfloat16, jnp.float32
    hbm, vmem = pl.BlockSpec(memory_space=ANY), pl.BlockSpec(memory_space=pltpu.VMEM)
    table = (2, 2, BINS // 32, 16, BINS)
    return pl.pallas_call(
        stack_body,
        out_shape=(
            jax.ShapeDtypeStruct((NTM, 3, 4, 2 * CH, KB), jnp.int16),
            jax.ShapeDtypeStruct((NTM, 16, KB), f32),
            jax.ShapeDtypeStruct((16, 128), f32),
            jax.ShapeDtypeStruct(table, bf),
            jax.ShapeDtypeStruct(table, bf),
        ),
        in_specs=[pl.BlockSpec(memory_space=pltpu.SMEM), hbm, vmem, vmem, vmem, vmem, vmem],
        out_specs=(hbm, hbm, vmem, hbm, hbm),
        scratch_shapes=[
            pltpu.VMEM((2, 4, 4, 2, SEG, BINS), bf),
            pltpu.VMEM((2, SRC, 4, 2, SEG, BINS), bf),
            pltpu.VMEM((2, 4, SRC, 2, SEG, BINS), bf),
            pltpu.VMEM((2, SRC, 2, SEG, BINS), bf),
            pltpu.VMEM((NTM * SEG, KB), bf),
            pltpu.VMEM((2, SRC, 2, NTM * SEG, KB), bf),
            pltpu.VMEM((ROWS, 256), bf),
            pltpu.VMEM((CH, 2, NTM * SEG, KB), bf),
            pltpu.VMEM((2, 16, ROWS, 256), bf),
            pltpu.VMEM((HALF * KB, 128), f32),
            pltpu.VMEM((HALF * KB, 128), f32),
            pltpu.VMEM((CH * KB, 128), f32),
            pltpu.VMEM((CH * KB, 128), f32),
            pltpu.VMEM((KB, 2 * CH, 256), bf),
            pltpu.VMEM((HALF * KB, 128), f32),
            pltpu.VMEM((SRC * CH, 128), f32),
            pltpu.VMEM((24, 4, 2 * CH, KB), jnp.int16),
            pltpu.VMEM((NTM, 16, KB), f32),
            pltpu.VMEM(table, bf),
            pltpu.VMEM(table, bf),
            pltpu.SemaphoreType.DMA((104,)),
            pltpu.SemaphoreType.DMA((104,)),
            pltpu.SemaphoreType.DMA((12,)),
            pltpu.SemaphoreType.DMA((24,)),
            pltpu.SemaphoreType.DMA((NTM, 3)),
            pltpu.SemaphoreType.DMA((3,)),
        ],
        compiler_params=pltpu.CompilerParams(
            collective_id=0, has_side_effects=True, vmem_limit_bytes=BIG
        ),
    )(plan, m, fl, *seeds)


def make_seeds():
    tau = np.arange(BINS)

    def pair(freq):
        angle = (np.multiply.outer(freq, tau) % (2 * BINS)) * (math.pi / BINS)
        return np.cos(angle), np.sin(angle)

    c1, s1 = pair(np.arange(BINS // 32) * 32)
    c2, s2 = pair(np.add.outer(np.arange(2), 2 * np.arange(16)))
    scale = 1.0 / math.sqrt(BINS)
    return [jnp.asarray(v, jnp.float32) for v in (c1, s1, c2 * scale, s2 * scale)]


def lags_body(v_ref, c_ref, inv_ref, th_ref, tl_ref, out_ref, xh, xl, factor):
    step = th_ref.shape[2]

    @pl.when(pl.program_id(0) == 0)
    def _():
        lane = lax.broadcasted_iota(jnp.int32, (CH, KB), 1)
        for j in range(NTM):
            factor[j] = (c_ref[j] * inv_ref[...]).T

        def split(q, carry):
            p, j = q // 4, lax.rem(q, 4)
            lanes = pl.ds(pl.multiple_of(q * KB, KB), KB)
            part = pl.ds(pl.multiple_of(p * CH, CH), CH)
            for s in range(12):
                rows = pl.ds(s * CH, CH)
                a, b = (
                    v_ref[2 * j + i, s, p].astype(jnp.int32).astype(jnp.float32)
                    * factor[2 * j + i, part, s : s + 1]
                    for i in range(2)
                )
                even = jnp.where(lane < KB // 2, a, pltpu.roll(b, KB // 2, 1))
                odd = jnp.where(lane < KB // 2, pltpu.roll(a, KB // 2, 1), b)
                for parity, value in enumerate((even, odd)):
                    high = value.astype(jnp.bfloat16)
                    xh[parity, rows, lanes] = high
                    xl[parity, rows, lanes] = (value - high.astype(jnp.float32)).astype(
                        jnp.bfloat16
                    )
            return carry

        lax.fori_loop(0, 2 * NTM // 2, split, 0)

    def dot(a, b):
        return jnp.dot(a, b, preferred_element_type=jnp.float32)

    even, odd = (
        dot(xl[i], th_ref[i]) + dot(xh[i], tl_ref[i]) + dot(xh[i], th_ref[i]) for i in range(2)
    )
    at = pl.program_id(0) * step
    out_ref[:, pl.ds(pl.multiple_of(at, step), step)] = even - odd
    out_ref[:, pl.ds(pl.multiple_of(at + BINS, step), step)] = even + odd


def lags(v, c, inv, th, tl):
    rows, step = 12 * CH, 256
    return pl.pallas_call(
        lags_body,
        grid=(BINS // step,),
        out_shape=jax.ShapeDtypeStruct((rows, 2 * BINS), jnp.float32),
        in_specs=[
            pl.BlockSpec((NTM, 12, 2, CH, KB), lambda g: (0, 0, 0, 0, 0)),
            pl.BlockSpec((NTM, 16, KB), lambda g: (0, 0, 0)),
            pl.BlockSpec((16, 128), lambda g: (0, 0)),
            pl.BlockSpec((2, BINS, step), lambda g: (0, 0, g)),
            pl.BlockSpec((2, BINS, step), lambda g: (0, 0, g)),
        ],
        out_specs=pl.BlockSpec((rows, 2 * BINS), lambda g: (0, 0)),
        scratch_shapes=[
            pltpu.VMEM((2, rows, BINS), jnp.bfloat16),
            pltpu.VMEM((2, rows, BINS), jnp.bfloat16),
            pltpu.VMEM((NTM, 128, 16), jnp.float32),
        ],
        compiler_params=pltpu.CompilerParams(vmem_limit_bytes=BIG),
    )(v, c, inv, th, tl)


def shards(spectra, quality, plan):
    flags = quality.astype(jnp.bfloat16)
    m = (spectra * flags[:, :, None, None]).transpose(0, 2, 1, 3)
    fl = jnp.pad(flags.T, ((0, 0), (0, KB - CH)))
    v, c, inv, th, tl = stack(plan, m, fl, make_seeds())
    th, tl = (t.reshape(2, BINS, BINS) for t in (th, tl))
    out = lags(v.reshape(NTM, 12, 2, CH, KB), c, inv, th, tl)
    return out.reshape(12, CH, 2 * BINS)


def solution(mesh):
    in_specs = (P("chan", "tm", None, None), P("chan", "tm"), P())
    out_specs = P("tm", "chan", None)
    return jax.shard_map(shards, mesh=mesh, in_specs=in_specs, out_specs=out_specs, check_vma=False)
```
